256 devices in a mesh: tm: 32 (over y, x, core), rows: 8 (over z).
Axes of the slice: x: 4, y: 4, z: 8, core: 2. Of those that a mesh axis runs over, the one named last changes fastest.
Arguments:
- frames_in: bfloat16 [128, 32, 32, 512], P('tm', 'rows'), may hold values from -6 to 6
- weight_in: bfloat16 [2, 512, 4608], P(None, 'rows'), may hold values from -0.09375 to 0.09375
- weight_out: bfloat16 [9, 2, 512, 512], P(None, None, 'rows'), may hold values from -0.015625 to 0.015625
- log_decay: float32 [512], replicated, may hold values from 7.8125e-05 to 0.06
- rotation: float32 [512], replicated, may hold values from -3.140625 to 3.140625
- start_state: float32 [32, 32, 2, 512], P('rows'), may hold values from -12 to 12
- skip_gain: float32 [512], replicated, may hold values from -1 to 1
Outputs:
- frames_out: bfloat16 [128, 32, 32, 512], P('tm', 'rows')
The draws below stay inside these ranges and needn't reach their ends.
All inputs are finite; a program needn't handle non-finite values.
Results may differ from the reference program's by a relative error of at most 0.0047.
Values may be sent and summed in bfloat16 or wider, within the bound.
No kernel may reach another device: no remote copies, remote signals or barrier semaphores. Data moves between devices by JAX's collectives and lax.ppermute only.
A program may use at most 64 MiB of HBM per device.

```python
import math
import jax
import jax.numpy as jnp
from jax import lax

D = 512
P_SIZE = 512
HH = 32
WW = 32
FRAMES = 128


def levels(stream_key, shape, pieces, smallest, largest):
    level, own = 1.0, jax.random.fold_in(stream_key, 6)
    for axis_at, blocks in pieces:
        steps = jnp.exp(jax.random.uniform(jax.random.fold_in(own, axis_at), (blocks,), jnp.float32, smallest / len(pieces), largest / len(pieces)))
        level = level * jnp.repeat(steps, shape[axis_at] // blocks).reshape([-1 if axis == axis_at else 1 for axis in range(len(shape))])
    return level


def noise(own_key, extent, scale, bound, pieces=(), dtype=jnp.bfloat16):
    gain = levels(own_key, extent, pieces, -0.22, 0.18) if pieces else 1.0
    array = jax.random.normal(own_key, extent, jnp.float32) * scale * gain
    return jnp.minimum(jnp.maximum(array, -bound), bound).astype(dtype)


def setup_inputs(seed: int = 0) -> dict:
    arg_keys = jax.random.split(jax.random.key(seed), 8)
    frames_in = noise(arg_keys[0], (FRAMES, HH, WW, D), 1.0, 6.0, ((0, 32), (1, 8)))
    weight_in = noise(arg_keys[1], (2, P_SIZE, 9 * D), (9 * D) ** -0.5, 0.09375, ((1, 8),))
    weight_out = noise(arg_keys[2], (9, 2, P_SIZE, D), (16 * 18 * P_SIZE) ** -0.5, 0.015625, ((2, 8),))
    log_decay = jnp.clip(jnp.exp(jax.random.uniform(arg_keys[3], (P_SIZE,), jnp.float32, math.log(7.812499825377017e-05), math.log(0.06))), 7.812499825377017e-05, 0.06)
    rotation = jnp.clip(jax.random.uniform(arg_keys[4], (P_SIZE,), jnp.float32, -3.140625, 3.140625), -3.140625, 3.140625)
    start_state = noise(arg_keys[5], (HH, WW, 2, P_SIZE), 2.0, 12.0, ((0, 8),), jnp.float32)
    skip_gain = jnp.clip(jax.random.uniform(arg_keys[6], (D,), jnp.float32, -1.0, 1.0), -1.0, 1.0)
    return {"frames_in": frames_in, "weight_in": weight_in, "weight_out": weight_out, "log_decay": log_decay, "rotation": rotation, "start_state": start_state, "skip_gain": skip_gain}


def conv_same(field, weight, channels):
    height = field.shape[0]
    columns = field.shape[1]
    padded = jnp.pad(field, ((1, 1), (1, 1), (0, 0)))
    summed = jnp.zeros((height, columns, weight.shape[0]), jnp.float32)
    for tap_index in range(9):
        row_shift = tap_index // 3
        col_shift = tap_index % 3
        window = padded[row_shift:row_shift + height, col_shift:col_shift + columns, :]
        weight_tap = weight[:, tap_index * channels:(tap_index + 1) * channels]
        summed = summed + lax.dot_general(window, weight_tap, (((2,), (1,)), ((), ())), preferred_element_type=jnp.float32)
    return summed


def reference(frames_in, weight_in, weight_out, log_decay, rotation, start_state, skip_gain):
    modulus = jnp.exp(-log_decay)
    lam_re = modulus * jnp.cos(rotation)
    lam_im = modulus * jnp.sin(rotation)
    matrix_in = weight_in.reshape(2 * P_SIZE, 9 * D)
    matrix_out = weight_out.reshape(18 * P_SIZE, D).T
    driven = lax.map(lambda single: conv_same(single, matrix_in, D), frames_in)

    def advance(carried, forcing):
        state_re, state_im = carried
        new_re = lam_re * state_re - lam_im * state_im + forcing[..., :P_SIZE]
        new_im = lam_re * state_im + lam_im * state_re + forcing[..., P_SIZE:]
        return (new_re, new_im), jnp.concatenate([new_re, new_im], -1).astype(jnp.bfloat16)

    _, held = lax.scan(advance, (start_state[:, :, 0, :], start_state[:, :, 1, :]), driven)
    mixing = lax.map(lambda single: conv_same(single, matrix_out, 2 * P_SIZE), held)
    pre_act = mixing + skip_gain * frames_in.astype(jnp.float32)
    return jax.nn.gelu(pre_act, approximate=False).astype(jnp.bfloat16)
```

```python
import functools

import jax
import jax.numpy as jnp
from jax import lax
from jax.experimental import pallas as pl
from jax.experimental.pallas import tpu as pltpu
from jax.sharding import Mesh, PartitionSpec as P

NY, NX, NC, NZ = 4, 4, 2, 8
F32, BF16 = jnp.float32, jnp.bfloat16
VMEM = pl.BlockSpec(memory_space=pltpu.VMEM)
SMEM = pl.BlockSpec(memory_space=pltpu.SMEM)
NT = (((1,), (1,)), ((), ()))
NN = (((1,), (0,)), ((), ()))


def call(body, out_shape, in_specs, flops, nbytes, scratch=()):
    return pl.pallas_call(
        body,
        out_shape=out_shape,
        in_specs=in_specs,
        out_specs=jax.tree.map(lambda _: VMEM, out_shape),
        scratch_shapes=list(scratch),
        compiler_params=pltpu.CompilerParams(vmem_limit_bytes=36 * 1024 * 1024),
        cost_estimate=pl.CostEstimate(flops=flops, bytes_accessed=nbytes, transcendentals=0),
    )


def shift(value, axis, steps, wrap=True):
    count = lax.axis_size(axis)
    pairs = [(i, (i + steps) % count) for i in range(count) if wrap or 0 <= i + steps < count]
    return lax.ppermute(value, axis, pairs)


def columns_shifted(summed):
    rows = summed[0].shape[0]
    column = lax.broadcasted_iota(jnp.int32, (rows, 1), 0) % 32
    left = jnp.where(column == 0, 0.0, pltpu.roll(summed[0], 1, 0))
    right = jnp.where(column == 31, 0.0, pltpu.roll(summed[2], rows - 1, 0))
    return left + summed[1] + right


def times(a_re, a_im, b_re, b_im):
    return a_re * b_re - a_im * b_im, a_re * b_im + a_im * b_re


def in_body(place, b0, b1, b2, b3, t0, t13, t2, d0, d13, d2, w_own, w_other, table, local, tails, ext):
    xi, ci = place[0], place[1]
    lam_re, lam_im = table[0, 0:1, :], table[1, 0:1, :]

    def work(low, high):
        for k, block in enumerate((b0, b1, b2, b3)):
            at = jnp.bitwise_and(xi - k + NX, NX - 1)
            top = (t0, t13.at[0:4], t2, t13.at[4:8])[k]
            down = (d0, d13.at[0:4], d2, d13.at[4:8])[k]
            ext[:, 0] = top[...]
            ext[:, 1:5] = block[...]
            ext[:, 5] = down[...]
            summed = []
            for b in range(3):
                total = None
                for a in range(3):
                    tap = 3 * a + b
                    cells = ext[:, a : a + 4].reshape(512, 512)
                    spans = [(tap * 512, 512)] if tap != 4 else [(2048, 256), (2304, 256)]
                    for first, width in spans:
                        ref, base = (low, 0) if first < 2304 else (high, 2304)
                        weight = ref[:, :, first - base : first - base + width].reshape(256, width)
                        part = lax.dot_general(
                            cells[:, first - tap * 512 : first - tap * 512 + width],
                            weight, NT, preferred_element_type=F32,
                        )
                        total = part if total is None else total + part
                summed.append(total)
            driven = columns_shifted(summed).reshape(4, 128, 256)
            re, im = driven[0, :, :128], driven[0, :, 128:]
            for f in range(4):
                if f:
                    up_re, up_im = times(lam_re, lam_im, re, im)
                    re, im = up_re + driven[f, :, :128], up_im + driven[f, :, 128:]
                local[at, f, :, :128] = re
                local[at, f, :, 128:] = im
            tails[at, :, :128] = re
            tails[at, :, 128:] = im

    @pl.when(ci == 0)
    def _():
        work(w_own, w_other)

    @pl.when(ci == 1)
    def _():
        work(w_other, w_own)


def chain_body(place, own, other, start, table, total, entry):
    ci, yi = place[1], place[2]
    lam_re, lam_im = table[0, 3:4, :], table[1, 3:4, :]
    first = yi == 0
    re = jnp.where(first, start[:, :128], 0.0)
    im = jnp.where(first, start[:, 128:], 0.0)
    low = ci == 0
    for x in range(NX):
        ours, theirs = own[x], other[x]
        before = (re, im)
        for c in range(NC):
            tail = jnp.where(low, ours, theirs) if c == 0 else jnp.where(low, theirs, ours)
            if c == 1:
                entry[x, :, :128] = jnp.where(low, before[0], re)
                entry[x, :, 128:] = jnp.where(low, before[1], im)
            up_re, up_im = times(lam_re, lam_im, re, im)
            re, im = up_re + tail[:, :128], up_im + tail[:, 128:]
    total[:, :128] = re.astype(BF16)
    total[:, 128:] = im.astype(BF16)


def held_body(local, entry, g1, g2, g3, table, held, first_row, last_row):
    def power(n):
        return table[0, n : n + 1, :], table[1, n : n + 1, :]

    re, im = g1[:, :128].astype(F32), g1[:, 128:].astype(F32)
    for g, n in ((g2, 4), (g3, 5)):
        more_re, more_im = times(*power(n), g[:, :128].astype(F32), g[:, 128:].astype(F32))
        re, im = re + more_re, im + more_im
    for x in range(NX):
        more_re, more_im = times(*power(6 + x), re, im)
        at_re, at_im = entry[x, :, :128] + more_re, entry[x, :, 128:] + more_im
        for f in range(4):
            up_re, up_im = times(*power(f), at_re, at_im)
            got_re = (local[x, f, :, :128] + up_re).astype(BF16)
            got_im = (local[x, f, :, 128:] + up_im).astype(BF16)
            held[x, f, :, :, :128] = got_re.reshape(4, 32, 128)
            held[x, f, :, :, 128:] = got_im.reshape(4, 32, 128)
            first_row[x, f, :, :128] = got_re[:32]
            first_row[x, f, :, 128:] = got_im[:32]
            last_row[x, f, :, :128] = got_re[96:]
            last_row[x, f, :, 128:] = got_im[96:]


def out_products(windows, w_own, w_other, ci, put):
    for ref, half in ((w_own, ci), (w_other, 1 - ci)):
        summed = []
        for b in range(3):
            total = None
            for a in range(3):
                weight = ref[3 * a + b].reshape(256, 256)
                part = lax.dot_general(windows[a], weight, NN, preferred_element_type=F32)
                total = part if total is None else total + part
            summed.append(total)
        put(pl.multiple_of(half * 256, 256), columns_shifted(summed))


def out_body(edges, place, held, *rest):
    if edges:
        top, down, w_own, w_other, p0, p1, p2, p3 = rest
    else:
        w_own, w_other, p0, p1, p2, p3 = rest
    xi, ci = place[0], place[1]
    for k, out in ((2, p2), (1, p1), (3, p3), (0, p0)):
        at = jnp.bitwise_and(xi + k, NX - 1)
        if edges:
            rows = [top[at][:, None], held[at, :, 0:1], held[at, :, 1:2], held[at, :, 2:3], held[at, :, 3:4], down[at][:, None]]
            windows = [jnp.concatenate([rows[a], rows[a + 3]], 1) for a in range(3)]
        else:
            windows = [held[at, :, a : a + 2] for a in range(3)]

        def put(first, value, out=out):
            out[:, :, :, pl.ds(first, 256)] = value.astype(out.dtype).reshape(4, 2, 32, 256)

        out_products([w.reshape(256, 256) for w in windows], w_own, w_other, ci, put)


def last_body(frames, gain, i0, i1, i2, i3, e0, e1, e2, e3, out):
    skip = gain[...]
    for row in range(4):
        parts = (i0, i1, i2, i3) if row in (1, 2) else (e0, e1, e2, e3)
        at = {0: 0, 3: 1, 1: 0, 2: 1}[row]
        for f in range(4):
            mixing = parts[0][f, at] + parts[1][f, at].astype(F32)
            mixing = mixing + parts[2][f, at].astype(F32) + parts[3][f, at].astype(F32)
            pre = mixing + skip * frames[f, row].astype(F32)
            out[f, row] = (0.5 * pre * (1.0 + lax.erf(pre * 0.7071067811865476))).astype(BF16)


def on_device(frames_in, weight_in, weight_out, log_decay, rotation, start_state, skip_gain):
    xi, ci, yi = lax.axis_index("x"), lax.axis_index("c"), lax.axis_index("y")
    place = jnp.stack([xi, ci, yi, 0]).astype(jnp.int32)

    def own_states(values, axis):
        shape = values.shape
        split = values.reshape(*shape[:axis], NZ, NX, 16, *shape[axis + 1 :])
        return lax.dynamic_index_in_dim(split, xi, axis + 1, keepdims=False)

    piece_in = lax.dynamic_slice(weight_in, (0, 16 * xi, 2304 * ci), (2, 16, 2304))
    piece_out = lax.dynamic_slice(weight_out, (0, 0, 16 * xi, 256 * ci), (9, 2, 16, 256))
    win_own = lax.all_gather(piece_in, "z", axis=1, tiled=True)
    wout_own = lax.all_gather(piece_out, "z", axis=2, tiled=True)

    b0 = frames_in
    b1, b3, b2 = shift(b0, "x", 1), shift(b0, "x", 3), shift(b0, "x", 2)
    t0, d0 = shift(b0[:, 3], "z", 1, False), shift(b0[:, 0], "z", -1, False)
    t13 = shift(jnp.concatenate([b1[:, 3], b3[:, 3]]), "z", 1, False)
    d13 = shift(jnp.concatenate([b1[:, 0], b3[:, 0]]), "z", -1, False)
    t2, d2 = shift(b2[:, 3], "z", 1, False), shift(b2[:, 0], "z", -1, False)

    decay = own_states(log_decay, 0).reshape(1, 128)
    angle = own_states(rotation, 0).reshape(1, 128)
    steps = jnp.array([1, 2, 3, 4, 32, 64, 0, 8, 16, 24, 0, 0, 0, 0, 0, 0], F32)
    later = jnp.array([0, 0, 0, 0, 0, 0, 4, 4, 4, 4, 0, 0, 0, 0, 0, 0], F32)
    steps = (steps + later * ci.astype(F32))[:, None]
    size = jnp.exp(-decay * steps)
    table = jnp.stack([size * jnp.cos(angle * steps), size * jnp.sin(angle * steps)])
    start = own_states(start_state, 3).reshape(128, 256)

    win_other = shift(win_own, "c", 1)
    local, tails = call(
        in_body,
        (jax.ShapeDtypeStruct((NX, 4, 128, 256), F32), jax.ShapeDtypeStruct((NX, 128, 256), F32)),
        [SMEM] + [VMEM] * 13,
        4_831_838_208, 10_000_000,
        [pltpu.VMEM((4, 6, 32, 512), BF16)],
    )(place, b0, b1, b2, b3, t0, t13, t2, d0, d13, d2, win_own, win_other, table)

    other_tails = shift(tails, "c", 1)
    total, entry = call(
        chain_body,
        (jax.ShapeDtypeStruct((128, 256), BF16), jax.ShapeDtypeStruct((NX, 128, 256), F32)),
        [SMEM] + [VMEM] * 4,
        4_000_000, 2_000_000,
    )(place, tails, other_tails, start, table)
    g1, g2, g3 = (shift(total, "y", k, False) for k in (1, 2, 3))
    row = jax.ShapeDtypeStruct((NX, 4, 32, 256), BF16)
    held, first_row, last_row = call(
        held_body,
        (jax.ShapeDtypeStruct((NX, 4, 4, 32, 256), BF16), row, row),
        [VMEM] * 6,
        8_000_000, 4_000_000,
    )(local, entry, g1, g2, g3, table)

    top, down = shift(last_row, "z", 1, False), shift(first_row, "z", -1, False)
    wout_other = shift(wout_own, "c", 1)
    half = (4, 2, 32, 512)
    parts = (jax.ShapeDtypeStruct(half, F32),) + (jax.ShapeDtypeStruct(half, BF16),) * 3
    i0, *inner = call(
        functools.partial(out_body, False), parts, [SMEM] + [VMEM] * 3, 2_415_919_104, 6_000_000
    )(place, held, wout_own, wout_other)
    inner = [shift(inner[k - 1], "x", k) for k in (1, 2, 3)]
    e0, *outer = call(
        functools.partial(out_body, True), parts, [SMEM] + [VMEM] * 5, 2_415_919_104, 6_000_000
    )(place, held, top, down, wout_own, wout_other)
    outer = [shift(outer[k - 1], "x", k) for k in (1, 2, 3)]
    return call(
        last_body,
        jax.ShapeDtypeStruct((4, 4, 32, 512), BF16),
        [VMEM] * 10,
        10_000_000, 5_000_000,
    )(frames_in, skip_gain.reshape(1, 512), i0, *inner, e0, *outer)


def solution(mesh):
    fine = Mesh(mesh.devices.reshape(NY, NX, NC, NZ), ("y", "x", "c", "z"))
    frames = P(("y", "x", "c"), "z", None, None)
    return jax.shard_map(
        on_device,
        mesh=fine,
        in_specs=(frames, P(None, "z", None), P(None, None, "z", None), P(), P(), P("z", None, None, None), P()),
        out_specs=frames,
        check_vma=False,
    )
```

```python
import functools

import jax
import jax.numpy as jnp
from jax import lax
from jax.experimental import pallas as pl
from jax.experimental.pallas import tpu as pltpu
from jax.sharding import Mesh, PartitionSpec as P

NY, NX, NC, NZ = 4, 4, 2, 8
F32, BF16 = jnp.float32, jnp.bfloat16
VMEM = pl.BlockSpec(memory_space=pltpu.VMEM)
HBM = pl.BlockSpec(memory_space=pltpu.HBM)
SMEM = pl.BlockSpec(memory_space=pltpu.SMEM)
NT = (((1,), (1,)), ((), ()))
NN = (((1,), (0,)), ((), ()))


def call(body, out_shape, in_specs, flops, nbytes, scratch=(), out_specs=None):
    if out_specs is None:
        out_specs = jax.tree.map(lambda _: VMEM, out_shape)
    out_shape = jax.tree.map(
        lambda shape, spec: pltpu.HBM(shape.shape, shape.dtype) if spec is HBM else shape, out_shape, out_specs
    )
    kernel = pl.pallas_call(
        body,
        out_shape=out_shape,
        in_specs=in_specs,
        out_specs=out_specs,
        scratch_shapes=list(scratch),
        compiler_params=pltpu.CompilerParams(vmem_limit_bytes=32 * 1024 * 1024),
        cost_estimate=pl.CostEstimate(flops=flops, bytes_accessed=nbytes, transcendentals=0),
    )

    def run(*values):
        return kernel(*[
            pltpu.with_memory_space_constraint(value, pltpu.HBM) if spec is HBM else value
            for value, spec in zip(values, in_specs)
        ])

    return run


def shift(value, axis, steps, wrap=True):
    count = lax.axis_size(axis)
    pairs = [(i, (i + steps) % count) for i in range(count) if wrap or 0 <= i + steps < count]
    return lax.ppermute(value, axis, pairs)


def columns_shifted(summed):
    rows = summed[0].shape[0]
    column = lax.broadcasted_iota(jnp.int32, (rows, 1), 0) % 32
    left = jnp.where(column == 0, 0.0, pltpu.roll(summed[0], 1, 0))
    right = jnp.where(column == 31, 0.0, pltpu.roll(summed[2], rows - 1, 0))
    return left + summed[1] + right


def copied(spans, sems):
    copies = [pltpu.make_async_copy(*span, sems.at[n]) for n, span in enumerate(spans)]
    for copy in copies:
        copy.start()
    for copy in copies:
        copy.wait()


def edge_body(frames, first_row, last_row):
    first_row[...] = frames[:, 0]
    last_row[...] = frames[:, 3]


def pair_body(top, down, out):
    out[0] = top[...]
    out[1] = down[...]


def states_body(place, start_state, rates, start, picked):
    source = lax.broadcasted_iota(jnp.int32, (512, 128), 0)
    lane = lax.broadcasted_iota(jnp.int32, (512, 128), 1)
    wanted = 64 * lax.shift_right_logical(lane, 4) + 16 * place[0] + jnp.bitwise_and(lane, 15)
    pick = (source == wanted).astype(F32)

    def of(value):
        return lax.dot_general(value, pick, NN, precision=lax.Precision.HIGHEST, preferred_element_type=F32)

    for part in range(2):
        start[:, part * 128 : part * 128 + 128] = of(start_state[:, :, part, :].reshape(128, 512))
    picked[...] = of(rates[...])


def pack_body(place, weight_in, weight_out, out, held, sems):
    rows = pl.ds(pl.multiple_of(16 * place[0], 16), 16)
    spans = [(weight_in.at[:, rows, pl.ds(pl.multiple_of(2304 * place[1], 128), 2304)], held.at[0:2])]
    half = pl.ds(pl.multiple_of(256 * place[1], 128), 256)
    for tap in range(9):
        spans.append((weight_out.at[tap, :, rows, half], held.at[2:4, :, tap * 256 : tap * 256 + 256]))
    copied(spans, sems)
    copied([(held, out)], sems)


def times(a_re, a_im, b_re, b_im):
    return a_re * b_re - a_im * b_im, a_re * b_im + a_im * b_re


def in_products(cells, weight, half):
    summed = []
    for b in range(3):
        total = None
        for a in range(3):
            tap = 3 * a + b
            first, last = max(tap * 512, 2304 * half), min(tap * 512 + 512, 2304 * half + 2304)
            if first >= last:
                continue
            window = cells[:, a : a + 4, :, first - tap * 512 : last - tap * 512].reshape(512, last - first)
            taps = weight[:, :, first - 2304 * half : last - 2304 * half].reshape(256, last - first)
            part = lax.dot_general(window, taps, NT, preferred_element_type=F32)
            total = part if total is None else total + part
        summed.append(total)
    return columns_shifted(summed)


def first_body(place, b0, b1, b2, b3, h0, h1, h2, h3, w_own, ext, part, weight, in_sems, w_sem):
    w_copy = pltpu.make_async_copy(w_own.at[0:2], weight, w_sem)
    w_copy.start()
    copies = []
    for k, (block, pair) in enumerate(zip((b0, b1, b2, b3), (h0, h1, h2, h3))):
        copies.append([
            pltpu.make_async_copy(block, ext.at[k, :, 1:5], in_sems.at[k, 0]),
            pltpu.make_async_copy(pair.at[0], ext.at[k, :, 0], in_sems.at[k, 1]),
            pltpu.make_async_copy(pair.at[1], ext.at[k, :, 5], in_sems.at[k, 2]),
        ])
        for copy in copies[-1]:
            copy.start()
    w_copy.wait()
    for k in range(NX):
        for copy in copies[k]:
            copy.wait()
        for half in range(2):

            @pl.when(place[1] == half)
            def _():
                part[k] = in_products(ext.at[k], weight, half)


def second_body(place, ext, part, w_other, start, table, local, tails):
    xi, ci, yi = place[0], place[1], place[2]
    lam_re, lam_im = table[0, 0:1, :], table[1, 0:1, :]
    weight = w_other.at[0:2]

    def work(half):
        for k in range(NX):
            at = jnp.bitwise_and(xi - k + NX, NX - 1)
            driven = (part[k] + in_products(ext.at[k], weight, half)).reshape(4, 128, 256)
            first = jnp.logical_and(at == 0, jnp.logical_and(ci == 0, yi == 0))
            re = jnp.where(first, start[:, :128], 0.0)
            im = jnp.where(first, start[:, 128:], 0.0)
            for f in range(4):
                up_re, up_im = times(lam_re, lam_im, re, im)
                re, im = up_re + driven[f, :, :128], up_im + driven[f, :, 128:]
                local[k, f, :, :128] = re
                local[k, f, :, 128:] = im
            tails[at, :, :128] = re
            tails[at, :, 128:] = im

    for half in range(2):

        @pl.when(ci == 1 - half)
        def _():
            work(half)


def chain_body(place, own, other, table, total, entry):
    ci = place[1]
    lam_re, lam_im = table[0, 3:4, :], table[1, 3:4, :]
    re = im = jnp.zeros((128, 128), F32)
    low = ci == 0
    for x in range(NX):
        ours, theirs = own[x], other[x]
        before = (re, im)
        for c in range(NC):
            tail = jnp.where(low, ours, theirs) if c == 0 else jnp.where(low, theirs, ours)
            if c == 1:
                entry[x, :, :128] = jnp.where(low, before[0], re)
                entry[x, :, 128:] = jnp.where(low, before[1], im)
            up_re, up_im = times(lam_re, lam_im, re, im)
            re, im = up_re + tail[:, :128], up_im + tail[:, 128:]
    total[:, :128] = re.astype(BF16)
    total[:, 128:] = im.astype(BF16)


def held_body(place, local, entry, g1, g2, g3, table, held, first_row, last_row):
    def power(n):
        return table[0, pl.ds(n, 1), :], table[1, pl.ds(n, 1), :]

    re, im = g1[:, :128].astype(F32), g1[:, 128:].astype(F32)
    for g, n in ((g2, 4), (g3, 5)):
        more_re, more_im = times(*power(n), g[:, :128].astype(F32), g[:, 128:].astype(F32))
        re, im = re + more_re, im + more_im
    for k in range(NX):
        x = jnp.bitwise_and(place[0] - k + NX, NX - 1)
        to = (NX - k) % NX
        more_re, more_im = times(*power(6 + x), re, im)
        at_re, at_im = entry[x, :, :128] + more_re, entry[x, :, 128:] + more_im
        for f in range(4):
            up_re, up_im = times(*power(f), at_re, at_im)
            got_re = (local[k, f, :, :128] + up_re).astype(BF16)
            got_im = (local[k, f, :, 128:] + up_im).astype(BF16)
            held[to, f, :, :, :128] = got_re.reshape(4, 32, 128)
            held[to, f, :, :, 128:] = got_im.reshape(4, 32, 128)
            first_row[to, f, :, :128] = got_re[:32]
            first_row[to, f, :, 128:] = got_im[:32]
            last_row[to, f, :, :128] = got_re[96:]
            last_row[to, f, :, 128:] = got_im[96:]


def out_body(edges, place, held, *rest):
    if edges:
        top, down, w_own, w_other, *outs = rest
        rows = [top[...][:, :, None], held[:, :, 0:1], held[:, :, 1:2], held[:, :, 2:3], held[:, :, 3:4], down[...][:, :, None]]
        windows = [jnp.concatenate([rows[a], rows[a + 3]], 2) for a in range(3)]
    else:
        w_own, w_other, *outs = rest
        windows = [held[:, :, a : a + 2] for a in range(3)]
    windows = [w.reshape(1024, 256) for w in windows]
    for ref, base, half in ((w_own, 2, place[1]), (w_other, 2, 1 - place[1])):
        first = pl.multiple_of(half * 256, 256)
        summed = []
        for b in range(3):
            total = None
            for a in range(3):
                tap = 3 * a + b
                weight = ref[base : base + 2, :, tap * 256 : tap * 256 + 256].reshape(256, 256)
                part = lax.dot_general(windows[a], weight, NN, preferred_element_type=F32)
                total = part if total is None else total + part
            summed.append(total)
        value = columns_shifted(summed).reshape(4, 4, 2, 32, 256)
        for k, out in enumerate(outs):
            out[:, :, :, pl.ds(first, 256)] = value[k].astype(out.dtype)


def last_body(frames, gain, i0, i1, i2, i3, e0, e1, e2, e3, out):
    skip = gain[...]
    for row in range(4):
        parts = (i0, i1, i2, i3) if row in (1, 2) else (e0, e1, e2, e3)
        at = {0: 0, 3: 1, 1: 0, 2: 1}[row]
        for f in range(4):
            mixing = parts[0][f, at] + parts[1][f, at].astype(F32)
            mixing = mixing + parts[2][f, at].astype(F32) + parts[3][f, at].astype(F32)
            pre = mixing + skip * frames[f, row].astype(F32)
            out[f, row] = (0.5 * pre * (1.0 + lax.erf(pre * 0.7071067811865476))).astype(BF16)


def on_device(frames_in, weight_in, weight_out, log_decay, rotation, start_state, skip_gain):
    xi, ci, yi = lax.axis_index("x"), lax.axis_index("c"), lax.axis_index("y")
    place = jnp.stack([xi, ci, yi, lax.axis_index("z")]).astype(jnp.int32)

    piece = call(
        pack_body, jax.ShapeDtypeStruct((4, 16, 2304), BF16), [SMEM, HBM, HBM], 0, 600_000,
        [pltpu.VMEM((4, 16, 2304), BF16), pltpu.SemaphoreType.DMA((10,))], HBM,
    )(place, weight_in, weight_out)
    w_own = lax.all_gather(piece, "z", axis=1, tiled=True)

    b0 = frames_in
    b1, b3, b2 = shift(b0, "x", 1), shift(b0, "x", 3), shift(b0, "x", 2)
    row = jax.ShapeDtypeStruct((4, 32, 512), BF16)
    first_row, last_row = call(edge_body, (row, row), [VMEM], 0, 600_000)(b0)
    t0, d0 = shift(last_row, "z", 1, False), shift(first_row, "z", -1, False)
    h0 = call(pair_body, jax.ShapeDtypeStruct((2, 4, 32, 512), BF16), [VMEM] * 2, 0, 500_000)(t0, d0)
    b1, b3, b2, h0 = lax.optimization_barrier((b1, b3, b2, h0))
    h1, h3, h2 = shift(h0, "x", 1), shift(h0, "x", 3), shift(h0, "x", 2)

    start, picked = call(
        states_body,
        (jax.ShapeDtypeStruct((128, 256), F32), jax.ShapeDtypeStruct((2, 128), F32)),
        [SMEM] + [VMEM] * 2, 40_000_000, 700_000,
    )(place, start_state, jnp.stack([log_decay, rotation]))
    steps = jnp.array([1, 2, 3, 4, 32, 64, 0, 8, 16, 24, 0, 0, 0, 0, 0, 0], F32)
    later = jnp.array([0, 0, 0, 0, 0, 0, 4, 4, 4, 4, 0, 0, 0, 0, 0, 0], F32)
    steps = (steps + later * ci.astype(F32))[:, None]
    size = jnp.exp(-picked[0:1] * steps)
    table = jnp.stack([size * jnp.cos(picked[1:2] * steps), size * jnp.sin(picked[1:2] * steps)])

    w_own, b1, b2, b3, h1, h2, h3, start, table = lax.optimization_barrier((w_own, b1, b2, b3, h1, h2, h3, start, table))
    w_other = shift(w_own, "c", 1)
    ext, part = call(
        first_body,
        (jax.ShapeDtypeStruct((NX, 4, 6, 32, 512), BF16), jax.ShapeDtypeStruct((NX, 512, 256), F32)),
        [SMEM] + [HBM] * 9,
        2_415_919_104, 9_000_000,
        [
            pltpu.VMEM((2, 128, 2304), BF16),
            pltpu.SemaphoreType.DMA((NX, 3)),
            pltpu.SemaphoreType.DMA(()),
        ],
    )(place, b0, b1, b2, b3, h0, h1, h2, h3, w_own)
    local, tails = call(
        second_body,
        (jax.ShapeDtypeStruct((NX, 4, 128, 256), F32), jax.ShapeDtypeStruct((NX, 128, 256), F32)),
        [SMEM] + [VMEM] * 5,
        2_415_919_104, 9_000_000,
    )(place, ext, part, w_other, start, table)

    other_tails = shift(tails, "c", 1)
    total, entry = call(
        chain_body,
        (jax.ShapeDtypeStruct((128, 256), BF16), jax.ShapeDtypeStruct((NX, 128, 256), F32)),
        [SMEM] + [VMEM] * 3,
        4_000_000, 2_000_000,
    )(place, tails, other_tails, table)
    g1, g2, g3 = (shift(total, "y", k, False) for k in (1, 2, 3))
    row = jax.ShapeDtypeStruct((NX, 4, 32, 256), BF16)
    held, first_row, last_row = call(
        held_body,
        (jax.ShapeDtypeStruct((NX, 4, 4, 32, 256), BF16), row, row),
        [SMEM] + [VMEM] * 6,
        8_000_000, 4_000_000,
    )(place, local, entry, g1, g2, g3, table)

    top, down = shift(last_row, "z", 1, False), shift(first_row, "z", -1, False)
    half = (4, 2, 32, 512)
    parts = (jax.ShapeDtypeStruct(half, F32),) + (jax.ShapeDtypeStruct(half, BF16),) * 3
    i0, *inner = call(
        functools.partial(out_body, False), parts, [SMEM] + [VMEM] * 3, 2_415_919_104, 6_000_000
    )(place, held, w_own, w_other)
    held, *inner = lax.optimization_barrier((held, *inner))
    inner = [shift(inner[k - 1], "x", k) for k in (1, 2, 3)]
    e0, *outer = call(
        functools.partial(out_body, True), parts, [SMEM] + [VMEM] * 5, 2_415_919_104, 6_000_000
    )(place, held, top, down, w_own, w_other)
    outer = [shift(outer[k - 1], "x", k) for k in (1, 2, 3)]
    return call(
        last_body,
        jax.ShapeDtypeStruct((4, 4, 32, 512), BF16),
        [VMEM] * 10,
        10_000_000, 5_000_000,
    )(frames_in, skip_gain.reshape(1, 512), i0, *inner, e0, *outer)


def solution(mesh):
    fine = Mesh(mesh.devices.reshape(NY, NX, NC, NZ), ("y", "x", "c", "z"))
    frames = P(("y", "x", "c"), "z", None, None)
    return jax.shard_map(
        on_device,
        mesh=fine,
        in_specs=(frames, P(None, "z", None), P(None, None, "z", None), P(), P(), P("z", None, None, None), P()),
        out_specs=frames,
        check_vma=False,
    )
```

```python
import functools

import jax
import jax.numpy as jnp
from jax import lax
from jax.experimental import pallas as pl
from jax.experimental.pallas import tpu as pltpu
from jax.sharding import Mesh, PartitionSpec as P

NY, NX, NC, NZ = 4, 4, 2, 8
F32, BF16 = jnp.float32, jnp.bfloat16
VMEM = pl.BlockSpec(memory_space=pltpu.VMEM)
HBM = pl.BlockSpec(memory_space=pltpu.HBM)
SMEM = pl.BlockSpec(memory_space=pltpu.SMEM)
SENT = (0, 1, 3, 2)
NT = (((1,), (1,)), ((), ()))
NN = (((1,), (0,)), ((), ()))


def call(body, out_shape, in_specs, flops, nbytes, scratch=(), out_specs=None):
    if out_specs is None:
        out_specs = jax.tree.map(lambda _: VMEM, out_shape)
    out_shape = jax.tree.map(
        lambda shape, spec: pltpu.HBM(shape.shape, shape.dtype) if spec is HBM else shape, out_shape, out_specs
    )
    kernel = pl.pallas_call(
        body,
        out_shape=out_shape,
        in_specs=in_specs,
        out_specs=out_specs,
        scratch_shapes=list(scratch),
        compiler_params=pltpu.CompilerParams(vmem_limit_bytes=24 * 1024 * 1024),
        cost_estimate=pl.CostEstimate(flops=flops, bytes_accessed=nbytes, transcendentals=0),
    )

    def run(*values):
        return kernel(*[
            pltpu.with_memory_space_constraint(value, pltpu.HBM) if spec is HBM else value
            for value, spec in zip(values, in_specs)
        ])

    return run


def shift(value, axis, steps, wrap=True):
    count = lax.axis_size(axis)
    pairs = [(i, (i + steps) % count) for i in range(count) if wrap or 0 <= i + steps < count]
    return lax.ppermute(value, axis, pairs)


def columns_shifted(summed):
    rows = summed[0].shape[0]
    column = lax.broadcasted_iota(jnp.int32, (rows, 1), 0) % 32
    left = jnp.where(column == 0, 0.0, pltpu.roll(summed[0], 1, 0))
    right = jnp.where(column == 31, 0.0, pltpu.roll(summed[2], rows - 1, 0))
    return left + summed[1] + right


def copied(spans, sems):
    copies = [pltpu.make_async_copy(*span, sems.at[n]) for n, span in enumerate(spans)]
    for copy in copies:
        copy.start()
    for copy in copies:
        copy.wait()


def edge_body(*refs):
    *blocks, first_rows, last_rows = refs
    for n, block in enumerate(blocks):
        first_rows[4 * n : 4 * n + 4] = block[:, 0]
        last_rows[4 * n : 4 * n + 4] = block[:, 3]


def frame_body(block, top, down, whole, pair):
    whole[:, 0] = top[...]
    whole[:, 1:5] = block[...]
    whole[:, 5] = down[...]
    pair[0] = top[...]
    pair[1] = down[...]


def tick_body(place, out):
    for n in range(4):
        out[n] = place[n]


def ordered(place, before, after):
    place, *_ = lax.optimization_barrier((place, *before))
    place = call(
        tick_body, jax.ShapeDtypeStruct((4,), jnp.int32), [SMEM], 10**11, 10**8, out_specs=SMEM
    )(place)
    return lax.optimization_barrier((place, *after))


def edges_of(*blocks):
    rows = jax.ShapeDtypeStruct((4 * len(blocks), 32, 512), BF16)
    first_rows, last_rows = call(edge_body, (rows, rows), [VMEM] * len(blocks), 0, 600_000)(*blocks)
    return shift(last_rows, "z", 1, False), shift(first_rows, "z", -1, False)


def states_body(place, start_state, rates, start, picked):
    source = lax.broadcasted_iota(jnp.int32, (512, 128), 0)
    lane = lax.broadcasted_iota(jnp.int32, (512, 128), 1)
    wanted = 64 * lax.shift_right_logical(lane, 4) + 16 * place[0] + jnp.bitwise_and(lane, 15)
    pick = (source == wanted).astype(F32)

    def of(value):
        return lax.dot_general(value, pick, NN, precision=lax.Precision.HIGHEST, preferred_element_type=F32)

    for part in range(2):
        start[:, part * 128 : part * 128 + 128] = of(start_state[:, :, part, :].reshape(128, 512))
    picked[...] = of(rates[...])


def pack_body(place, weight_in, weight_out, out, sems):
    rows = pl.ds(pl.multiple_of(16 * place[0], 16), 16)
    half = pl.ds(pl.multiple_of(256 * place[1], 128), 256)
    spans = [
        (weight_out.at[tap, :, rows, half], out.at[2:4, :, tap * 256 : tap * 256 + 256]) for tap in range(9)
    ]
    spans.append((weight_in.at[:, rows, pl.ds(pl.multiple_of(2304 * place[1], 128), 2304)], out.at[0:2]))
    copied(spans, sems)


def place_body(first, place, *refs):
    *pieces, out = refs
    for k, piece in enumerate(pieces):
        at = jnp.bitwise_and(place[3] - k + NZ, NZ - 1)
        begin = first if piece.shape[0] == 4 else 0
        for part in range(2):
            out[part, at] = piece[begin + part]


def placed(first, place, pieces):
    out = jax.ShapeDtypeStruct((2, NZ, 16, 2304), BF16)
    body = functools.partial(place_body, first)
    return call(body, out, [SMEM] + [VMEM] * 8, 0, 2_400_000)(place, *pieces).reshape(2, 128, 2304)


def times(a_re, a_im, b_re, b_im):
    return a_re * b_re - a_im * b_im, a_re * b_im + a_im * b_re


def in_products(cells, weight, half):
    summed = []
    for b in range(3):
        total = None
        for a in range(3):
            tap = 3 * a + b
            first, last = max(tap * 512, 2304 * half), min(tap * 512 + 512, 2304 * half + 2304)
            if first >= last:
                continue
            window = cells[:, a : a + 4, :, first - tap * 512 : last - tap * 512].reshape(512, last - first)
            taps = weight[:, :, first - 2304 * half : last - 2304 * half].reshape(256, last - first)
            part = lax.dot_general(window, taps, NT, preferred_element_type=F32)
            total = part if total is None else total + part
        summed.append(total)
    return columns_shifted(summed)


def first_body(place, e0, e1, b2, h2, e3, weight, e2, part):
    e2[:, 0] = h2[0]
    e2[:, 1:5] = b2[...]
    e2[:, 5] = h2[1]
    for k, cells in enumerate((e0, e1, e2, e3)):
        for half in range(2):

            @pl.when(place[1] == half)
            def _():
                part[k] = in_products(cells, weight, half)


def second_body(place, e0, e1, e2, e3, part, weight, start, table, local, tails):
    xi, ci, yi = place[0], place[1], place[2]
    lam_re, lam_im = table[0, 0:1, :], table[1, 0:1, :]

    def work(half):
        for k, cells in enumerate((e0, e1, e2, e3)):
            at = jnp.bitwise_and(xi - k + NX, NX - 1)
            driven = (part[k] + in_products(cells, weight, half)).reshape(4, 128, 256)
            first = jnp.logical_and(at == 0, jnp.logical_and(ci == 0, yi == 0))
            re = jnp.where(first, start[:, :128], 0.0)
            im = jnp.where(first, start[:, 128:], 0.0)
            for f in range(4):
                up_re, up_im = times(lam_re, lam_im, re, im)
                re, im = up_re + driven[f, :, :128], up_im + driven[f, :, 128:]
                local[k, f, :, :128] = re
                local[k, f, :, 128:] = im
            tails[at, :, :128] = re
            tails[at, :, 128:] = im

    for half in range(2):

        @pl.when(ci == 1 - half)
        def _():
            work(half)


def chain_body(place, own, other, table, total, entry):
    ci = place[1]
    lam_re, lam_im = table[0, 3:4, :], table[1, 3:4, :]
    re = im = jnp.zeros((128, 128), F32)
    low = ci == 0
    for x in range(NX):
        ours, theirs = own[x], other[x]
        before = (re, im)
        for c in range(NC):
            tail = jnp.where(low, ours, theirs) if c == 0 else jnp.where(low, theirs, ours)
            if c == 1:
                entry[x, :, :128] = jnp.where(low, before[0], re)
                entry[x, :, 128:] = jnp.where(low, before[1], im)
            up_re, up_im = times(lam_re, lam_im, re, im)
            re, im = up_re + tail[:, :128], up_im + tail[:, 128:]
    total[:, :128] = re.astype(BF16)
    total[:, 128:] = im.astype(BF16)


def held_body(place, local, entry, g1, g2, g3, table, held, first_row, last_row):
    def power(n):
        return table[0, pl.ds(n, 1), :], table[1, pl.ds(n, 1), :]

    re, im = g1[:, :128].astype(F32), g1[:, 128:].astype(F32)
    for g, n in ((g2, 4), (g3, 5)):
        more_re, more_im = times(*power(n), g[:, :128].astype(F32), g[:, 128:].astype(F32))
        re, im = re + more_re, im + more_im
    for k in range(NX):
        x = jnp.bitwise_and(place[0] - k + NX, NX - 1)
        to = SENT.index((NX - k) % NX)
        more_re, more_im = times(*power(6 + x), re, im)
        at_re, at_im = entry[x, :, :128] + more_re, entry[x, :, 128:] + more_im
        for f in range(4):
            up_re, up_im = times(*power(f), at_re, at_im)
            got_re = (local[k, f, :, :128] + up_re).astype(BF16)
            got_im = (local[k, f, :, 128:] + up_im).astype(BF16)
            held[to, f, :, :, :128] = got_re.reshape(4, 32, 128)
            held[to, f, :, :, 128:] = got_im.reshape(4, 32, 128)
            first_row[to, f, :, :128] = got_re[:32]
            first_row[to, f, :, 128:] = got_im[:32]
            last_row[to, f, :, :128] = got_re[96:]
            last_row[to, f, :, 128:] = got_im[96:]


def out_windows(edges, held, top, down, blocks):
    if edges:
        rows = [top[blocks][:, :, None]] + [held[blocks, :, n : n + 1] for n in range(4)] + [down[blocks][:, :, None]]
        windows = [jnp.concatenate([rows[a], rows[a + 3]], 2) for a in range(3)]
    else:
        windows = [held[blocks, :, a : a + 2] for a in range(3)]
    return [w.reshape(-1, 256) for w in windows]


def out_store(windows, place, w_own, w_other, outs):
    for ref, half in ((w_own, place[1]), (w_other, 1 - place[1])):
        first = pl.multiple_of(half * 256, 256)
        summed = []
        for b in range(3):
            total = None
            for a in range(3):
                tap = 3 * a + b
                weight = ref[:, :, tap * 256 : tap * 256 + 256].reshape(256, 256)
                part = lax.dot_general(windows[a], weight, NN, preferred_element_type=F32)
                total = part if total is None else total + part
            summed.append(total)
        value = columns_shifted(summed).reshape(-1, 4, 2, 32, 256)
        for k, out in enumerate(outs):
            out[:, :, :, pl.ds(first, 256)] = value[k].astype(out.dtype)


def inner_body(blocks, place, held, w_own, w_other, *outs):
    out_store(out_windows(False, held, None, None, blocks), place, w_own, w_other, outs)


def edge_out_body(place, held, top, down, w_own, w_other, *outs):
    out_store(out_windows(True, held, top, down, slice(1, 4)), place, w_own, w_other, outs)


def own_body(place, held, top, down, w_own, w_other, *outs):
    own = slice(0, 1)
    pairs = zip(out_windows(False, held, top, down, own), out_windows(True, held, top, down, own))
    out_store([jnp.concatenate(pair) for pair in pairs], place, w_own, w_other, outs)


def last_body(frames, gain, i0, i1, i2, i3, e0, e1, e2, e3, out):
    skip = gain[...]
    for row in range(4):
        parts = (i0, i1, i2, i3) if row in (1, 2) else (e0, e1, e2, e3)
        at = {0: 0, 3: 1, 1: 0, 2: 1}[row]
        for f in range(4):
            mixing = parts[0][f, at] + parts[1][f, at].astype(F32)
            mixing = mixing + parts[2][f, at].astype(F32) + parts[3][f, at].astype(F32)
            pre = mixing + skip * frames[f, row].astype(F32)
            out[f, row] = (0.5 * pre * (1.0 + lax.erf(pre * 0.7071067811865476))).astype(BF16)


def on_device(frames_in, weight_in, weight_out, log_decay, rotation, start_state, skip_gain):
    xi, ci, yi = lax.axis_index("x"), lax.axis_index("c"), lax.axis_index("y")
    place = jnp.stack([xi, ci, yi, lax.axis_index("z")]).astype(jnp.int32)

    piece = call(
        pack_body, jax.ShapeDtypeStruct((4, 16, 2304), BF16), [SMEM, HBM, HBM], 0, 600_000,
        [pltpu.SemaphoreType.DMA((10,))],
    )(place, weight_in, weight_out)
    t0, d0 = edges_of(frames_in)
    up1, down1 = shift(piece, "z", 1), shift(piece, "z", -1)
    b2 = shift(frames_in, "x", 2)
    whole = jax.ShapeDtypeStruct((4, 6, 32, 512), BF16)
    e0, h0 = call(
        frame_body, (whole, jax.ShapeDtypeStruct((2, 4, 32, 512), BF16)), [VMEM] * 3, 0, 1_500_000
    )(frames_in, t0, d0)
    e1, e3 = shift(e0, "x", 1), shift(e0, "x", 3)
    place, up1, down1 = ordered(place, (up1, down1), (up1, down1))
    up2, down2 = shift(up1, "z", 1), shift(down1, "z", -1)
    start, picked = call(
        states_body,
        (jax.ShapeDtypeStruct((128, 256), F32), jax.ShapeDtypeStruct((2, 128), F32)),
        [SMEM] + [VMEM] * 2, 40_000_000, 700_000,
    )(place, start_state, jnp.stack([log_decay, rotation]))
    steps = jnp.array([1, 2, 3, 4, 32, 64, 0, 8, 16, 24, 0, 0, 0, 0, 0, 0], F32)
    later = jnp.array([0, 0, 0, 0, 0, 0, 4, 4, 4, 4, 0, 0, 0, 0, 0, 0], F32)
    steps = (steps + later * ci.astype(F32))[:, None]
    size = jnp.exp(-picked[0:1] * steps)
    table = jnp.stack([size * jnp.cos(picked[1:2] * steps), size * jnp.sin(picked[1:2] * steps)])
    place, up2, down2, b2, h0, start, table = ordered(place, (up2, down2, b2, start, table), (up2, down2, b2, h0, start, table))
    up3, down3 = shift(up2, "z", 1), shift(down2, "z", -1)
    h2 = shift(h0, "x", 2)
    up4, down4 = shift(up3[0:2], "z", 1), shift(down3[2:4], "z", -1)

    up4, down4, h2, e1, e3 = lax.optimization_barrier((up4, down4, h2, e1, e3))
    near = (down3, down2, down1)
    win_own = placed(0, place, (piece, up1, up2, up3, up4, *near))
    win_other = shift(win_own, "c", 1)
    e2, part = call(
        first_body,
        (whole, jax.ShapeDtypeStruct((NX, 512, 256), F32)),
        [SMEM] + [VMEM] * 6,
        2_415_919_104, 9_000_000,
    )(place, e0, e1, b2, h2, e3, win_own)
    local, tails = call(
        second_body,
        (jax.ShapeDtypeStruct((NX, 4, 128, 256), F32), jax.ShapeDtypeStruct((NX, 128, 256), F32)),
        [SMEM] + [VMEM] * 8,
        2_415_919_104, 9_000_000,
    )(place, e0, e1, e2, e3, part, win_other, start, table)

    other_tails = shift(tails, "c", 1)
    total, entry = call(
        chain_body,
        (jax.ShapeDtypeStruct((128, 256), BF16), jax.ShapeDtypeStruct((NX, 128, 256), F32)),
        [SMEM] + [VMEM] * 3,
        4_000_000, 2_000_000,
    )(place, tails, other_tails, table)
    g1, g2, g3 = (shift(total, "y", k, False) for k in (1, 2, 3))
    total, down4 = lax.optimization_barrier((total, down4))
    wout_own = placed(2, place, (piece, up1, up2, up3, down4, *near))
    g1, g2, g3, wout_own = lax.optimization_barrier((g1, g2, g3, wout_own))
    wout_other = shift(wout_own, "c", 1)
    row = jax.ShapeDtypeStruct((NX, 4, 32, 256), BF16)
    held, first_row, last_row = call(
        held_body,
        (jax.ShapeDtypeStruct((NX, 4, 4, 32, 256), BF16), row, row),
        [SMEM] + [VMEM] * 6,
        8_000_000, 4_000_000,
    )(place, local, entry, g1, g2, g3, table)

    half = (4, 2, 32, 512)

    def out_call(body, count, dtype, specs, flops):
        return call(
            body, (jax.ShapeDtypeStruct(half, dtype),) * count, [SMEM] + [VMEM] * specs, flops, flops // 600
        )

    block = 603_979_776
    top, down = shift(last_row, "z", 1, False), shift(first_row, "z", -1, False)
    inner = out_call(functools.partial(inner_body, slice(1, 4)), 3, BF16, 3, 3 * block)(
        place, held, wout_own, wout_other
    )
    *inner, held = lax.optimization_barrier((*inner, held))
    inner = [shift(value, "x", k) for k, value in zip(SENT[1:], inner)]
    outer = out_call(edge_out_body, 3, BF16, 5, 30 * block)(place, held, top, down, wout_own, wout_other)
    *outer, held = lax.optimization_barrier((*outer, held))
    outer = [shift(value, "x", k) for k, value in zip(SENT[1:], outer)]
    *inner, held = lax.optimization_barrier((*inner, held))
    i0, e0 = out_call(own_body, 2, F32, 5, 0)(place, held, top, down, wout_own, wout_other)
    return call(
        last_body,
        jax.ShapeDtypeStruct((4, 4, 32, 512), BF16),
        [VMEM] * 10,
        10_000_000, 5_000_000,
    )(frames_in, skip_gain.reshape(1, 512), i0, *inner, e0, *outer)


def solution(mesh):
    fine = Mesh(mesh.devices.reshape(NY, NX, NC, NZ), ("y", "x", "c", "z"))
    frames = P(("y", "x", "c"), "z", None, None)
    return jax.shard_map(
        on_device,
        mesh=fine,
        in_specs=(frames, P(None, "z", None), P(None, None, "z", None), P(), P(), P("z", None, None, None), P()),
        out_specs=frames,
        check_vma=False,
    )
```

```python
import functools

import jax
import jax.numpy as jnp
from jax import lax
from jax.experimental import pallas as pl
from jax.experimental.pallas import tpu as pltpu
from jax.sharding import Mesh, PartitionSpec as P

NY, NX, NC, NZ = 4, 4, 2, 8
F32, BF16 = jnp.float32, jnp.bfloat16
VMEM = pl.BlockSpec(memory_space=pltpu.VMEM)
HBM = pl.BlockSpec(memory_space=pltpu.HBM)
SENT = (0, 1, 3, 2)
NT = (((1,), (1,)), ((), ()))
NN = (((1,), (0,)), ((), ()))


def call(body, out_shape, in_specs, flops, nbytes, scratch=(), out_specs=None):
    if out_specs is None:
        out_specs = jax.tree.map(lambda _: VMEM, out_shape)
    out_shape = jax.tree.map(
        lambda shape, spec: pltpu.HBM(shape.shape, shape.dtype) if spec is HBM else shape, out_shape, out_specs
    )
    kernel = pl.pallas_call(
        body,
        out_shape=out_shape,
        in_specs=in_specs,
        out_specs=out_specs,
        scratch_shapes=list(scratch),
        compiler_params=pltpu.CompilerParams(vmem_limit_bytes=24 * 1024 * 1024),
        cost_estimate=pl.CostEstimate(flops=flops, bytes_accessed=nbytes, transcendentals=0),
    )

    def run(*values):
        return kernel(*[
            pltpu.with_memory_space_constraint(value, pltpu.HBM) if spec is HBM else value
            for value, spec in zip(values, in_specs)
        ])

    return run


def position():
    return tuple(lax.axis_index(axis) for axis in ("x", "c", "y", "z"))


def shift(value, axis, steps, wrap=True):
    count = lax.axis_size(axis)
    pairs = [(i, (i + steps) % count) for i in range(count) if wrap or 0 <= i + steps < count]
    return lax.ppermute(value, axis, pairs)


def columns_shifted(summed):
    rows = summed[0].shape[0]
    column = lax.broadcasted_iota(jnp.int32, (rows, 1), 0) % 32
    left = jnp.where(column == 0, 0.0, pltpu.roll(summed[0], 1, 0))
    right = jnp.where(column == 31, 0.0, pltpu.roll(summed[2], rows - 1, 0))
    return left + summed[1] + right


def copied(spans, sems):
    copies = [pltpu.make_async_copy(*span, sems.at[n]) for n, span in enumerate(spans)]
    for copy in copies:
        copy.start()
    for copy in copies:
        copy.wait()


def edge_body(*refs):
    *blocks, first_rows, last_rows = refs
    for n, block in enumerate(blocks):
        first_rows[4 * n : 4 * n + 4] = block[:, 0]
        last_rows[4 * n : 4 * n + 4] = block[:, 3]


def frame_body(block, top, down, whole, pair):
    whole[:, 0] = top[...]
    whole[:, 1:5] = block[...]
    whole[:, 5] = down[...]
    pair[0] = top[...]
    pair[1] = down[...]


def tick_body(token, out):
    out[...] = token[...]


def ordered(token, before, after):
    token, *_ = lax.optimization_barrier((token, *before))
    token = call(tick_body, jax.ShapeDtypeStruct((8, 128), F32), [VMEM], 10**11, 10**8)(token)
    return lax.optimization_barrier((token, *after))


def edges_of(*blocks):
    rows = jax.ShapeDtypeStruct((4 * len(blocks), 32, 512), BF16)
    first_rows, last_rows = call(edge_body, (rows, rows), [VMEM] * len(blocks), 0, 600_000)(*blocks)
    return shift(last_rows, "z", 1, False), shift(first_rows, "z", -1, False)


def states_body(start_state, rates, start, picked):
    place = position()
    source = lax.broadcasted_iota(jnp.int32, (512, 128), 0)
    lane = lax.broadcasted_iota(jnp.int32, (512, 128), 1)
    wanted = 64 * lax.shift_right_logical(lane, 4) + 16 * place[0] + jnp.bitwise_and(lane, 15)
    pick = (source == wanted).astype(F32)

    def of(value):
        return lax.dot_general(value, pick, NN, precision=lax.Precision.HIGHEST, preferred_element_type=F32)

    for part in range(2):
        start[:, part * 128 : part * 128 + 128] = of(start_state[:, :, part, :].reshape(128, 512))
    picked[...] = of(rates[...])


def pack_body(weight_in, weight_out, out, sems):
    place = position()
    rows = pl.ds(pl.multiple_of(16 * place[0], 16), 16)
    half = pl.ds(pl.multiple_of(256 * place[1], 128), 256)
    spans = [
        (weight_out.at[tap, :, rows, half], out.at[2:4, :, tap * 256 : tap * 256 + 256]) for tap in range(9)
    ]
    spans.append((weight_in.at[:, rows, pl.ds(pl.multiple_of(2304 * place[1], 128), 2304)], out.at[0:2]))
    copied(spans, sems)


def place_body(first, *refs):
    place = position()
    *pieces, out = refs
    for k, piece in enumerate(pieces):
        at = jnp.bitwise_and(place[3] - k + NZ, NZ - 1)
        begin = first if piece.shape[0] == 4 else 0
        for part in range(2):
            out[part, at] = piece[begin + part]


def placed(first, pieces):
    out = jax.ShapeDtypeStruct((2, NZ, 16, 2304), BF16)
    body = functools.partial(place_body, first)
    return call(body, out, [VMEM] * 8, 0, 2_400_000)(*pieces).reshape(2, 128, 2304)


def times(a_re, a_im, b_re, b_im):
    return a_re * b_re - a_im * b_im, a_re * b_im + a_im * b_re


def in_products(cells, weight, half):
    summed = []
    for b in range(3):
        total = None
        for a in range(3):
            tap = 3 * a + b
            first, last = max(tap * 512, 2304 * half), min(tap * 512 + 512, 2304 * half + 2304)
            if first >= last:
                continue
            window = cells[:, a : a + 4, :, first - tap * 512 : last - tap * 512].reshape(512, last - first)
            taps = weight[:, :, first - 2304 * half : last - 2304 * half].reshape(256, last - first)
            part = lax.dot_general(window, taps, NT, preferred_element_type=F32)
            total = part if total is None else total + part
        summed.append(total)
    return columns_shifted(summed)


def first_body(e0, e1, b2, h2, e3, weight, _, ext, part, sems):
    place = position()
    copies = {
        k: pltpu.make_async_copy(block, ext.at[k], sems.at[k]) for k, block in ((0, e0), (1, e1), (3, e3))
    }
    for copy in copies.values():
        copy.start()
    ext[2, :, 0] = h2[0]
    ext[2, :, 1:5] = b2[...]
    ext[2, :, 5] = h2[1]
    for k in (2, 0, 1, 3):
        if k in copies:
            copies[k].wait()
        for half in range(2):

            @pl.when(place[1] == half)
            def _():
                part[k] = in_products(ext.at[k], weight, half)


def second_body(ext, part, weight, start, table, local, tails):
    place = position()
    xi, ci, yi = place[0], place[1], place[2]
    lam_re, lam_im = table[0, 0:1, :], table[1, 0:1, :]

    def work(half):
        for k in range(NX):
            cells = ext.at[k]
            at = jnp.bitwise_and(xi - k + NX, NX - 1)
            driven = (part[k] + in_products(cells, weight, half)).reshape(4, 128, 256)
            first = jnp.logical_and(at == 0, jnp.logical_and(ci == 0, yi == 0))
            re = jnp.where(first, start[:, :128], 0.0)
            im = jnp.where(first, start[:, 128:], 0.0)
            for f in range(4):
                up_re, up_im = times(lam_re, lam_im, re, im)
                re, im = up_re + driven[f, :, :128], up_im + driven[f, :, 128:]
                local[k, f, :, :128] = re
                local[k, f, :, 128:] = im
            tails[at, :, :128] = re
            tails[at, :, 128:] = im

    for half in range(2):

        @pl.when(ci == 1 - half)
        def _():
            work(half)


def chain_body(own, other, table, total, entry):
    place = position()
    ci = place[1]
    lam_re, lam_im = table[0, 3:4, :], table[1, 3:4, :]
    re = im = jnp.zeros((128, 128), F32)
    low = ci == 0
    for x in range(NX):
        ours, theirs = own[x], other[x]
        before = (re, im)
        for c in range(NC):
            tail = jnp.where(low, ours, theirs) if c == 0 else jnp.where(low, theirs, ours)
            if c == 1:
                entry[x, :, :128] = jnp.where(low, before[0], re)
                entry[x, :, 128:] = jnp.where(low, before[1], im)
            up_re, up_im = times(lam_re, lam_im, re, im)
            re, im = up_re + tail[:, :128], up_im + tail[:, 128:]
    total[:, :128] = re.astype(BF16)
    total[:, 128:] = im.astype(BF16)


def held_body(local, entry, g1, g2, g3, table, held, first_row, last_row):
    place = position()
    def power(n):
        return table[0, pl.ds(n, 1), :], table[1, pl.ds(n, 1), :]

    re, im = g1[:, :128].astype(F32), g1[:, 128:].astype(F32)
    for g, n in ((g2, 4), (g3, 5)):
        more_re, more_im = times(*power(n), g[:, :128].astype(F32), g[:, 128:].astype(F32))
        re, im = re + more_re, im + more_im
    for k in range(NX):
        x = jnp.bitwise_and(place[0] - k + NX, NX - 1)
        to = SENT.index((NX - k) % NX)
        more_re, more_im = times(*power(6 + x), re, im)
        at_re, at_im = entry[x, :, :128] + more_re, entry[x, :, 128:] + more_im
        for f in range(4):
            up_re, up_im = times(*power(f), at_re, at_im)
            got_re = (local[k, f, :, :128] + up_re).astype(BF16)
            got_im = (local[k, f, :, 128:] + up_im).astype(BF16)
            held[to, f, :, :, :128] = got_re.reshape(4, 32, 128)
            held[to, f, :, :, 128:] = got_im.reshape(4, 32, 128)
            first_row[to, f, :, :128] = got_re[:32]
            first_row[to, f, :, 128:] = got_im[:32]
            last_row[to, f, :, :128] = got_re[96:]
            last_row[to, f, :, 128:] = got_im[96:]


def out_windows(edges, held, top, down, blocks):
    if edges:
        rows = [top[blocks][:, :, None]] + [held[blocks, :, n : n + 1] for n in range(4)] + [down[blocks][:, :, None]]
        windows = [jnp.concatenate([rows[a], rows[a + 3]], 2) for a in range(3)]
    else:
        windows = [held[blocks, :, a : a + 2] for a in range(3)]
    return [w.reshape(-1, 256) for w in windows]


def out_store(windows, w_own, w_other, outs):
    place = position()
    for ref, half in ((w_own, place[1]), (w_other, 1 - place[1])):
        first = pl.multiple_of(half * 256, 256)
        summed = []
        for b in range(3):
            total = None
            for a in range(3):
                tap = 3 * a + b
                weight = ref[:, :, tap * 256 : tap * 256 + 256].reshape(256, 256)
                part = lax.dot_general(windows[a], weight, NN, preferred_element_type=F32)
                total = part if total is None else total + part
            summed.append(total)
        value = columns_shifted(summed).reshape(-1, 4, 2, 32, 256)
        for k, out in enumerate(outs):
            out[:, :, :, pl.ds(first, 256)] = value[k].astype(out.dtype)


def inner_body(blocks, held, w_own, w_other, *outs):
    out_store(out_windows(False, held, None, None, blocks), w_own, w_other, outs)


def edge_out_body(held, top, down, w_own, w_other, *outs):
    out_store(out_windows(True, held, top, down, slice(1, 4)), w_own, w_other, outs)


def activated(mixing, skip, frames):
    pre = mixing + skip * frames.astype(F32)
    return (0.5 * pre * (1.0 + lax.erf(pre * 0.7071067811865476))).astype(BF16)


def own_body(held, top, down, w_own, w_other, frames, gain, i1, i2, i3, inner, edge, own):
    blocks = slice(0, 1)
    pairs = zip(out_windows(False, held, top, down, blocks), out_windows(True, held, top, down, blocks))
    out_store([jnp.concatenate(pair) for pair in pairs], w_own, w_other, (own, edge))
    skip = gain[...]
    for f in range(4):
        for row in range(2):
            mixing = own[f, row] + i1[f, row].astype(F32) + i2[f, row].astype(F32) + i3[f, row].astype(F32)
            inner[f, row] = activated(mixing, skip, frames[f, row + 1])


def last_body(frames, gain, inner, e0, e1, e2, e3, out):
    skip = gain[...]
    for f in range(4):
        out[f, 1:3] = inner[f]
        for row in range(2):
            mixing = e0[f, row] + e1[f, row].astype(F32) + e2[f, row].astype(F32) + e3[f, row].astype(F32)
            out[f, 3 * row] = activated(mixing, skip, frames[f, 3 * row])


def on_device(frames_in, weight_in, weight_out, log_decay, rotation, start_state, skip_gain):
    ci = lax.axis_index("c")
    piece = call(
        pack_body, jax.ShapeDtypeStruct((4, 16, 2304), BF16), [HBM, HBM], 0, 600_000,
        [pltpu.SemaphoreType.DMA((10,))],
    )(weight_in, weight_out)
    t0, d0 = edges_of(frames_in)
    up1, down1 = shift(piece, "z", 1), shift(piece, "z", -1)
    b2 = shift(frames_in, "x", 2)
    whole = jax.ShapeDtypeStruct((4, 6, 32, 512), BF16)
    e0, h0 = call(
        frame_body, (whole, jax.ShapeDtypeStruct((2, 4, 32, 512), BF16)), [VMEM] * 3, 0, 1_500_000
    )(frames_in, t0, d0)
    e1, e3 = shift(e0, "x", 1), shift(e0, "x", 3)
    token, up1, down1 = ordered(jnp.zeros((8, 128), F32), (up1, down1), (up1, down1))
    up2, down2 = shift(up1, "z", 1), shift(down1, "z", -1)
    start, picked = call(
        states_body,
        (jax.ShapeDtypeStruct((128, 256), F32), jax.ShapeDtypeStruct((2, 128), F32)),
        [VMEM] * 2, 40_000_000, 700_000,
    )(start_state, jnp.stack([log_decay, rotation]))
    steps = jnp.array([1, 2, 3, 4, 32, 64, 0, 8, 16, 24, 0, 0, 0, 0, 0, 0], F32)
    later = jnp.array([0, 0, 0, 0, 0, 0, 4, 4, 4, 4, 0, 0, 0, 0, 0, 0], F32)
    steps = (steps + later * ci.astype(F32))[:, None]
    size = jnp.exp(-picked[0:1] * steps)
    table = jnp.stack([size * jnp.cos(picked[1:2] * steps), size * jnp.sin(picked[1:2] * steps)])
    token, up2, down2, b2, h0, start, table = ordered(token, (up2, down2, b2, start, table), (up2, down2, b2, h0, start, table))
    up3, down3 = shift(up2, "z", 1), shift(down2, "z", -1)
    h2 = shift(h0, "x", 2)
    up4, down4 = shift(up3[0:2], "z", 1), shift(down3[2:4], "z", -1)

    up4, down4, h2, e1, e3 = lax.optimization_barrier((up4, down4, h2, e1, e3))
    near = (down3, down2, down1)
    win_own = placed(0, (piece, up1, up2, up3, up4, *near))
    win_other = shift(win_own, "c", 1)
    ext, part = call(
        first_body,
        (jax.ShapeDtypeStruct((NX, 4, 6, 32, 512), BF16), jax.ShapeDtypeStruct((NX, 512, 256), F32)),
        [HBM, HBM, VMEM, VMEM, HBM, VMEM, VMEM],
        2_415_919_104, 9_000_000,
        [pltpu.SemaphoreType.DMA((NX,))],
    )(e0, e1, b2, h2, e3, win_own, token)
    local, tails = call(
        second_body,
        (jax.ShapeDtypeStruct((NX, 4, 128, 256), F32), jax.ShapeDtypeStruct((NX, 128, 256), F32)),
        [VMEM] * 5,
        2_415_919_104, 9_000_000,
    )(ext, part, win_other, start, table)

    other_tails = shift(tails, "c", 1)
    total, entry = call(
        chain_body,
        (jax.ShapeDtypeStruct((128, 256), BF16), jax.ShapeDtypeStruct((NX, 128, 256), F32)),
        [VMEM] * 3,
        4_000_000, 2_000_000,
    )(tails, other_tails, table)
    g1, g2, g3 = (shift(total, "y", k, False) for k in (1, 2, 3))
    total, down4 = lax.optimization_barrier((total, down4))
    wout_own = placed(2, (piece, up1, up2, up3, down4, *near))
    g1, g2, g3, wout_own = lax.optimization_barrier((g1, g2, g3, wout_own))
    wout_other = shift(wout_own, "c", 1)
    row = jax.ShapeDtypeStruct((NX, 4, 32, 256), BF16)
    held, first_row, last_row = call(
        held_body,
        (jax.ShapeDtypeStruct((NX, 4, 4, 32, 256), BF16), row, row),
        [VMEM] * 6,
        8_000_000, 4_000_000,
    )(local, entry, g1, g2, g3, table)

    half = (4, 2, 32, 512)

    def out_call(body, count, dtype, specs, flops):
        return call(
            body, (jax.ShapeDtypeStruct(half, dtype),) * count, [VMEM] * specs, flops, flops // 600
        )

    block = 603_979_776
    top, down = shift(last_row, "z", 1, False), shift(first_row, "z", -1, False)
    inner = out_call(functools.partial(inner_body, slice(1, 4)), 3, BF16, 3, 3 * block)(
        held, wout_own, wout_other
    )
    *inner, held = lax.optimization_barrier((*inner, held))
    inner = [shift(value, "x", k) for k, value in zip(SENT[1:], inner)]
    outer = out_call(edge_out_body, 3, BF16, 5, 30 * block)(held, top, down, wout_own, wout_other)
    *outer, held = lax.optimization_barrier((*outer, held))
    outer = [shift(value, "x", k) for k, value in zip(SENT[1:], outer)]
    *inner, held = lax.optimization_barrier((*inner, held))
    gain = skip_gain.reshape(1, 512)
    done, edge = call(
        own_body,
        (jax.ShapeDtypeStruct(half, BF16), jax.ShapeDtypeStruct(half, F32)),
        [VMEM] * 10, 0, 0,
        [pltpu.VMEM(half, F32)],
    )(held, top, down, wout_own, wout_other, frames_in, gain, *inner)
    return call(
        last_body,
        jax.ShapeDtypeStruct((4, 4, 32, 512), BF16),
        [VMEM] * 7,
        10_000_000, 5_000_000,
    )(frames_in, gain, done, edge, *outer)


def solution(mesh):
    fine = Mesh(mesh.devices.reshape(NY, NX, NC, NZ), ("y", "x", "c", "z"))
    frames = P(("y", "x", "c"), "z", None, None)
    return jax.shard_map(
        on_device,
        mesh=fine,
        in_specs=(frames, P(None, "z", None), P(None, None, "z", None), P(), P(), P("z", None, None, None), P()),
        out_specs=frames,
        check_vma=False,
    )
```

```python
import functools

import jax
import jax.numpy as jnp
from jax import lax
from jax.experimental import pallas as pl
from jax.experimental.pallas import tpu as pltpu
from jax.sharding import Mesh, PartitionSpec as P

NY, NX, NC, NZ = 4, 4, 2, 8
F32, BF16 = jnp.float32, jnp.bfloat16
VMEM = pl.BlockSpec(memory_space=pltpu.VMEM)
HBM = pl.BlockSpec(memory_space=pltpu.HBM)
ANY = pl.BlockSpec(memory_space=pl.ANY)
SENT = (0, 1, 3, 2)
NT = (((1,), (1,)), ((), ()))
NN = (((1,), (0,)), ((), ()))


def call(body, out_shape, in_specs, flops, nbytes, scratch=(), out_specs=None):
    if out_specs is None:
        out_specs = jax.tree.map(lambda _: VMEM, out_shape)
    out_shape = jax.tree.map(
        lambda shape, spec: pltpu.HBM(shape.shape, shape.dtype) if spec is HBM else shape, out_shape, out_specs
    )
    kernel = pl.pallas_call(
        body,
        out_shape=out_shape,
        in_specs=in_specs,
        out_specs=out_specs,
        scratch_shapes=list(scratch),
        compiler_params=pltpu.CompilerParams(vmem_limit_bytes=24 * 1024 * 1024),
        cost_estimate=pl.CostEstimate(flops=flops, bytes_accessed=nbytes, transcendentals=0),
    )

    def run(*values):
        return kernel(*[
            pltpu.with_memory_space_constraint(value, pltpu.HBM) if spec is HBM else value
            for value, spec in zip(values, in_specs)
        ])

    return run


def position():
    return tuple(lax.axis_index(axis) for axis in ("x", "c", "y", "z"))


def shift(value, axis, steps, wrap=True):
    count = lax.axis_size(axis)
    pairs = [(i, (i + steps) % count) for i in range(count) if wrap or 0 <= i + steps < count]
    return lax.ppermute(value, axis, pairs)


def columns_shifted(summed):
    rows = summed[0].shape[0]
    column = lax.broadcasted_iota(jnp.int32, (rows, 1), 0) % 32
    left = jnp.where(column == 0, 0.0, pltpu.roll(summed[0], 1, 0))
    right = jnp.where(column == 31, 0.0, pltpu.roll(summed[2], rows - 1, 0))
    return left + summed[1] + right


def copied(spans, sems):
    copies = [pltpu.make_async_copy(*span, sems.at[n]) for n, span in enumerate(spans)]
    for copy in copies:
        copy.start()
    for copy in copies:
        copy.wait()


def edge_body(*refs):
    *blocks, first_rows, last_rows = refs
    for n, block in enumerate(blocks):
        first_rows[4 * n : 4 * n + 4] = block[:, 0]
        last_rows[4 * n : 4 * n + 4] = block[:, 3]


def frame_body(block, top, down, whole, pair):
    whole[:, 0] = top[...]
    whole[:, 1:5] = block[...]
    whole[:, 5] = down[...]
    pair[0] = top[...]
    pair[1] = down[...]


def tick_body(token, out):
    out[...] = token[...]


def ordered(token, before, after):
    token, *_ = lax.optimization_barrier((token, *before))
    token = call(tick_body, jax.ShapeDtypeStruct((8, 128), F32), [VMEM], 10**11, 10**8)(token)
    return lax.optimization_barrier((token, *after))


def edges_of(*blocks):
    rows = jax.ShapeDtypeStruct((4 * len(blocks), 32, 512), BF16)
    first_rows, last_rows = call(edge_body, (rows, rows), [VMEM] * len(blocks), 0, 600_000)(*blocks)
    return shift(last_rows, "z", 1, False), shift(first_rows, "z", -1, False)


def states_body(start_state, rates, start, picked):
    place = position()
    source = lax.broadcasted_iota(jnp.int32, (512, 128), 0)
    lane = lax.broadcasted_iota(jnp.int32, (512, 128), 1)
    wanted = 64 * lax.shift_right_logical(lane, 4) + 16 * place[0] + jnp.bitwise_and(lane, 15)
    pick = (source == wanted).astype(F32)

    def of(value):
        return lax.dot_general(value, pick, NN, precision=lax.Precision.HIGHEST, preferred_element_type=F32)

    for part in range(2):
        start[:, part * 128 : part * 128 + 128] = of(start_state[:, :, part, :].reshape(128, 512))
    picked[...] = of(rates[...])


def pack_body(weight_in, weight_out, out, sems):
    place = position()
    rows = pl.ds(pl.multiple_of(16 * place[0], 16), 16)
    half = pl.ds(pl.multiple_of(256 * place[1], 128), 256)
    spans = [
        (weight_out.at[tap, :, rows, half], out.at[2:4, :, tap * 256 : tap * 256 + 256]) for tap in range(9)
    ]
    spans.append((weight_in.at[:, rows, pl.ds(pl.multiple_of(2304 * place[1], 128), 2304)], out.at[0:2]))
    copied(spans, sems)


def place_body(first, *refs):
    place = position()
    *pieces, out = refs
    for k, piece in enumerate(pieces):
        at = jnp.bitwise_and(place[3] - k + NZ, NZ - 1)
        begin = first if piece.shape[0] == 4 else 0
        for part in range(2):
            out[part, at] = piece[begin + part]


def placed(first, pieces):
    out = jax.ShapeDtypeStruct((2, NZ, 16, 2304), BF16)
    body = functools.partial(place_body, first)
    return call(body, out, [VMEM] * 8, 0, 0)(*pieces).reshape(2, 128, 2304)


def times(a_re, a_im, b_re, b_im):
    return a_re * b_re - a_im * b_im, a_re * b_im + a_im * b_re


def in_products(cells, weight, half):
    summed = []
    for b in range(3):
        total = None
        for a in range(3):
            tap = 3 * a + b
            first, last = max(tap * 512, 2304 * half), min(tap * 512 + 512, 2304 * half + 2304)
            if first >= last:
                continue
            window = cells[:, a : a + 4, :, first - tap * 512 : last - tap * 512].reshape(512, last - first)
            taps = weight[:, :, first - 2304 * half : last - 2304 * half].reshape(256, last - first)
            part = lax.dot_general(window, taps, NT, preferred_element_type=F32)
            total = part if total is None else total + part
        summed.append(total)
    return columns_shifted(summed)


def ahead_body(e0, weight, _, part):
    place = position()
    for half in range(2):

        @pl.when(place[1] == half)
        def _():
            part[...] = in_products(e0, weight, half)


def first_body(e0, e1, b2, h2, e3, weight, ahead, _, ext, part, sems):
    place = position()
    copies = {
        k: pltpu.make_async_copy(block, ext.at[k], sems.at[k]) for k, block in ((1, e1), (3, e3), (0, e0))
    }
    copies[2] = pltpu.make_async_copy(b2, ext.at[2, :, 1:5], sems.at[2])
    for copy in copies.values():
        copy.start()
    part[0] = ahead[...]
    ext[2, :, 0] = h2[0]
    ext[2, :, 5] = h2[1]
    for k in (1, 3, 2):
        copies[k].wait()
        for half in range(2):

            @pl.when(place[1] == half)
            def _():
                part[k] = in_products(ext.at[k], weight, half)

    copies[0].wait()


def second_body(ext, part, weight, start, table, local, tails):
    place = position()
    xi, ci, yi = place[0], place[1], place[2]
    lam_re, lam_im = table[0, 0:1, :], table[1, 0:1, :]

    def work(half):
        for k in range(NX):
            cells = ext.at[k]
            at = jnp.bitwise_and(xi - k + NX, NX - 1)
            driven = (part[k] + in_products(cells, weight, half)).reshape(4, 128, 256)
            first = jnp.logical_and(at == 0, jnp.logical_and(ci == 0, yi == 0))
            re = jnp.where(first, start[:, :128], 0.0)
            im = jnp.where(first, start[:, 128:], 0.0)
            for f in range(4):
                up_re, up_im = times(lam_re, lam_im, re, im)
                re, im = up_re + driven[f, :, :128], up_im + driven[f, :, 128:]
                local[k, f, :, :128] = re
                local[k, f, :, 128:] = im
            tails[at, :, :128] = re
            tails[at, :, 128:] = im

    for half in range(2):

        @pl.when(ci == 1 - half)
        def _():
            work(half)


def chain_body(own, other, table, total, entry):
    place = position()
    ci = place[1]
    lam_re, lam_im = table[0, 3:4, :], table[1, 3:4, :]
    re = im = jnp.zeros((128, 128), F32)
    low = ci == 0
    for x in range(NX):
        ours, theirs = own[x], other[x]
        before = (re, im)
        for c in range(NC):
            tail = jnp.where(low, ours, theirs) if c == 0 else jnp.where(low, theirs, ours)
            if c == 1:
                entry[x, :, :128] = jnp.where(low, before[0], re)
                entry[x, :, 128:] = jnp.where(low, before[1], im)
            up_re, up_im = times(lam_re, lam_im, re, im)
            re, im = up_re + tail[:, :128], up_im + tail[:, 128:]
    total[:, :128] = re.astype(BF16)
    total[:, 128:] = im.astype(BF16)


def held_body(local, entry, g1, g2, g3, table, held, first_row, last_row):
    place = position()
    def power(n):
        return table[0, pl.ds(n, 1), :], table[1, pl.ds(n, 1), :]

    re, im = g1[:, :128].astype(F32), g1[:, 128:].astype(F32)
    for g, n in ((g2, 4), (g3, 5)):
        more_re, more_im = times(*power(n), g[:, :128].astype(F32), g[:, 128:].astype(F32))
        re, im = re + more_re, im + more_im
    for k in range(NX):
        x = jnp.bitwise_and(place[0] - k + NX, NX - 1)
        to = SENT.index((NX - k) % NX)
        more_re, more_im = times(*power(6 + x), re, im)
        at_re, at_im = entry[x, :, :128] + more_re, entry[x, :, 128:] + more_im
        for f in range(4):
            up_re, up_im = times(*power(f), at_re, at_im)
            got_re = (local[k, f, :, :128] + up_re).astype(BF16)
            got_im = (local[k, f, :, 128:] + up_im).astype(BF16)
            held[to, f, :, :, :128] = got_re.reshape(4, 32, 128)
            held[to, f, :, :, 128:] = got_im.reshape(4, 32, 128)
            first_row[to, f, :, :128] = got_re[:32]
            first_row[to, f, :, 128:] = got_im[:32]
            last_row[to, f, :, :128] = got_re[96:]
            last_row[to, f, :, 128:] = got_im[96:]


def out_windows(edges, held, top, down, blocks):
    if edges:
        rows = [top[blocks][:, :, None]] + [held[blocks, :, n : n + 1] for n in range(4)] + [down[blocks][:, :, None]]
        windows = [jnp.concatenate([rows[a], rows[a + 3]], 2) for a in range(3)]
    else:
        windows = [held[blocks, :, a : a + 2] for a in range(3)]
    return [w.reshape(-1, 256) for w in windows]


def out_store(windows, w_own, w_other, outs):
    place = position()
    for ref, half in ((w_own, place[1]), (w_other, 1 - place[1])):
        first = pl.multiple_of(half * 256, 256)
        summed = []
        for b in range(3):
            total = None
            for a in range(3):
                tap = 3 * a + b
                weight = ref[:, :, tap * 256 : tap * 256 + 256].reshape(256, 256)
                part = lax.dot_general(windows[a], weight, NN, preferred_element_type=F32)
                total = part if total is None else total + part
            summed.append(total)
        value = columns_shifted(summed).reshape(-1, 4, 2, 32, 256)
        for k, out in enumerate(outs):
            out[:, :, :, pl.ds(first, 256)] = value[k].astype(out.dtype)


def inner_body(blocks, held, w_own, w_other, *outs):
    out_store(out_windows(False, held, None, None, blocks), w_own, w_other, outs)


def edge_out_body(held, top, down, w_own, w_other, *outs):
    out_store(out_windows(True, held, top, down, slice(1, 4)), w_own, w_other, outs)


def activated(mixing, skip, frames):
    pre = mixing + skip * frames.astype(F32)
    return (0.5 * pre * (1.0 + lax.erf(pre * 0.7071067811865476))).astype(BF16)


def own_body(held, top, down, w_own, w_other, frames, gain, i1, i2, i3, inner, edge, own):
    blocks = slice(0, 1)
    pairs = zip(out_windows(False, held, top, down, blocks), out_windows(True, held, top, down, blocks))
    out_store([jnp.concatenate(pair) for pair in pairs], w_own, w_other, (own, edge))
    skip = gain[...]
    for f in range(4):
        for row in range(2):
            mixing = own[f, row] + i1[f, row].astype(F32) + i2[f, row].astype(F32) + i3[f, row].astype(F32)
            inner[f, row] = activated(mixing, skip, frames[f, row + 1])


def last_body(frames, gain, inner, e0, e1, e2, e3, out):
    skip = gain[...]
    for f in range(4):
        out[f, 1:3] = inner[f]
        for row in range(2):
            mixing = e0[f, row] + e1[f, row].astype(F32) + e2[f, row].astype(F32) + e3[f, row].astype(F32)
            out[f, 3 * row] = activated(mixing, skip, frames[f, 3 * row])


def on_device(frames_in, weight_in, weight_out, log_decay, rotation, start_state, skip_gain):
    ci = lax.axis_index("c")
    piece = call(
        pack_body, jax.ShapeDtypeStruct((4, 16, 2304), BF16), [HBM, HBM], 0, 600_000,
        [pltpu.SemaphoreType.DMA((10,))],
    )(weight_in, weight_out)
    t0, d0 = edges_of(frames_in)
    up1, down1 = shift(piece, "z", 1), shift(piece, "z", -1)
    b2 = shift(frames_in, "x", 2)
    whole = jax.ShapeDtypeStruct((4, 6, 32, 512), BF16)
    e0, h0 = call(
        frame_body, (whole, jax.ShapeDtypeStruct((2, 4, 32, 512), BF16)), [VMEM] * 3, 0, 1_500_000
    )(frames_in, t0, d0)
    e1, e3 = shift(e0, "x", 1), shift(e0, "x", 3)
    token, up1, down1 = ordered(jnp.zeros((8, 128), F32), (up1, down1), (up1, down1))
    up2, down2 = shift(up1, "z", 1), shift(down1, "z", -1)
    start, picked = call(
        states_body,
        (jax.ShapeDtypeStruct((128, 256), F32), jax.ShapeDtypeStruct((2, 128), F32)),
        [VMEM] * 2, 40_000_000, 700_000,
    )(start_state, jnp.stack([log_decay, rotation]))
    steps = jnp.array([1, 2, 3, 4, 32, 64, 0, 8, 16, 24, 0, 0, 0, 0, 0, 0], F32)
    later = jnp.array([0, 0, 0, 0, 0, 0, 4, 4, 4, 4, 0, 0, 0, 0, 0, 0], F32)
    steps = (steps + later * ci.astype(F32))[:, None]
    size = jnp.exp(-picked[0:1] * steps)
    table = jnp.stack([size * jnp.cos(picked[1:2] * steps), size * jnp.sin(picked[1:2] * steps)])
    token, up2, down2, b2, h0, start, table = ordered(token, (up2, down2, b2, start, table), (up2, down2, b2, h0, start, table))
    up3, down3 = shift(up2, "z", 1), shift(down2, "z", -1)
    h2 = shift(h0, "x", 2)
    up4, down4 = shift(up3[0:2], "z", 1), shift(down3[2:4], "z", -1)

    up4, down4 = lax.optimization_barrier((up4, down4))
    near = (down3, down2, down1)
    win_own = placed(0, (piece, up1, up2, up3, up4, *near))
    win_other = shift(win_own, "c", 1)
    ahead = call(
        ahead_body, jax.ShapeDtypeStruct((512, 256), F32), [VMEM] * 3, 0, 0
    )(e0, win_own, token)
    token, ahead, e1, e3, h2 = ordered(token, (ahead, e1, e3, h2), (ahead, e1, e3, h2))
    ext, part = call(
        first_body,
        (jax.ShapeDtypeStruct((NX, 4, 6, 32, 512), BF16), jax.ShapeDtypeStruct((NX, 512, 256), F32)),
        [ANY, ANY, ANY, VMEM, ANY, VMEM, VMEM, VMEM],
        2_415_919_104, 9_000_000,
        [pltpu.SemaphoreType.DMA((NX,))],
    )(e0, e1, b2, h2, e3, win_own, ahead, token)
    local, tails = call(
        second_body,
        (jax.ShapeDtypeStruct((NX, 4, 128, 256), F32), jax.ShapeDtypeStruct((NX, 128, 256), F32)),
        [VMEM] * 5,
        2_415_919_104, 9_000_000,
    )(ext, part, win_other, start, table)

    other_tails = shift(tails, "c", 1)
    total, entry = call(
        chain_body,
        (jax.ShapeDtypeStruct((128, 256), BF16), jax.ShapeDtypeStruct((NX, 128, 256), F32)),
        [VMEM] * 3,
        4_000_000, 2_000_000,
    )(tails, other_tails, table)
    g1, g2, g3 = (shift(total, "y", k, False) for k in (1, 2, 3))
    total, down4 = lax.optimization_barrier((total, down4))
    wout_own = placed(2, (piece, up1, up2, up3, down4, *near))
    g1, g2, g3, wout_own = lax.optimization_barrier((g1, g2, g3, wout_own))
    wout_other = shift(wout_own, "c", 1)
    row = jax.ShapeDtypeStruct((NX, 4, 32, 256), BF16)
    held, first_row, last_row = call(
        held_body,
        (jax.ShapeDtypeStruct((NX, 4, 4, 32, 256), BF16), row, row),
        [VMEM] * 6,
        8_000_000, 4_000_000,
    )(local, entry, g1, g2, g3, table)

    half = (4, 2, 32, 512)

    def out_call(body, count, dtype, specs, flops):
        return call(
            body, (jax.ShapeDtypeStruct(half, dtype),) * count, [VMEM] * specs, flops, flops // 600
        )

    block = 603_979_776
    top, down = shift(last_row, "z", 1, False), shift(first_row, "z", -1, False)
    inner = out_call(functools.partial(inner_body, slice(1, 4)), 3, BF16, 3, 3 * block)(
        held, wout_own, wout_other
    )
    *inner, held = lax.optimization_barrier((*inner, held))
    inner = [shift(value, "x", k) for k, value in zip(SENT[1:], inner)]
    outer = out_call(edge_out_body, 3, BF16, 5, 30 * block)(held, top, down, wout_own, wout_other)
    *outer, held = lax.optimization_barrier((*outer, held))
    outer = [shift(value, "x", k) for k, value in zip(SENT[1:], outer)]
    *inner, held = lax.optimization_barrier((*inner, held))
    gain = skip_gain.reshape(1, 512)
    done, edge = call(
        own_body,
        (jax.ShapeDtypeStruct(half, BF16), jax.ShapeDtypeStruct(half, F32)),
        [VMEM] * 10, 0, 0,
        [pltpu.VMEM(half, F32)],
    )(held, top, down, wout_own, wout_other, frames_in, gain, *inner)
    return call(
        last_body,
        jax.ShapeDtypeStruct((4, 4, 32, 512), BF16),
        [VMEM] * 7,
        10_000_000, 5_000_000,
    )(frames_in, gain, done, edge, *outer)


def solution(mesh):
    fine = Mesh(mesh.devices.reshape(NY, NX, NC, NZ), ("y", "x", "c", "z"))
    frames = P(("y", "x", "c"), "z", None, None)
    return jax.shard_map(
        on_device,
        mesh=fine,
        in_specs=(frames, P(None, "z", None), P(None, None, "z", None), P(), P(), P("z", None, None, None), P()),
        out_specs=frames,
        check_vma=False,
    )
```

```python
import functools

import jax
import jax.numpy as jnp
from jax import lax
from jax.experimental import pallas as pl
from jax.experimental.pallas import tpu as pltpu
from jax.sharding import Mesh, PartitionSpec as P

NY, NX, NC, NZ = 4, 4, 2, 8
F32, BF16 = jnp.float32, jnp.bfloat16
VMEM = pl.BlockSpec(memory_space=pltpu.VMEM)
HBM = pl.BlockSpec(memory_space=pltpu.HBM)
ANY = pl.BlockSpec(memory_space=pl.ANY)
SENT = (0, 2, 1, 3)
NT = (((1,), (1,)), ((), ()))
NN = (((1,), (0,)), ((), ()))


def call(body, out_shape, in_specs, flops, nbytes, scratch=(), out_specs=None):
    if out_specs is None:
        out_specs = jax.tree.map(lambda _: VMEM, out_shape)
    out_shape = jax.tree.map(
        lambda shape, spec: pltpu.HBM(shape.shape, shape.dtype) if spec is HBM else shape, out_shape, out_specs
    )
    kernel = pl.pallas_call(
        body,
        out_shape=out_shape,
        in_specs=in_specs,
        out_specs=out_specs,
        scratch_shapes=list(scratch),
        compiler_params=pltpu.CompilerParams(vmem_limit_bytes=24 * 1024 * 1024),
        cost_estimate=pl.CostEstimate(flops=flops, bytes_accessed=nbytes, transcendentals=0),
    )

    def run(*values):
        return kernel(*[
            pltpu.with_memory_space_constraint(value, pltpu.HBM) if spec is HBM else value
            for value, spec in zip(values, in_specs)
        ])

    return run


def position():
    return tuple(lax.axis_index(axis) for axis in ("x", "c", "y", "z"))


def shift(value, axis, steps, wrap=True):
    count = lax.axis_size(axis)
    pairs = [(i, (i + steps) % count) for i in range(count) if wrap or 0 <= i + steps < count]
    return lax.ppermute(value, axis, pairs)


def columns_shifted(summed):
    rows = summed[0].shape[0]
    column = lax.broadcasted_iota(jnp.int32, (rows, 1), 0) % 32
    left = jnp.where(column == 0, 0.0, pltpu.roll(summed[0], 1, 0))
    right = jnp.where(column == 31, 0.0, pltpu.roll(summed[2], rows - 1, 0))
    return left + summed[1] + right


def copied(spans, sems):
    copies = [pltpu.make_async_copy(*span, sems.at[n]) for n, span in enumerate(spans)]
    for copy in copies:
        copy.start()
    for copy in copies:
        copy.wait()


def edge_body(*refs):
    *blocks, first_rows, last_rows = refs
    for n, block in enumerate(blocks):
        first_rows[4 * n : 4 * n + 4] = block[:, 0]
        last_rows[4 * n : 4 * n + 4] = block[:, 3]


def frame_body(block, top, down, whole, pair):
    whole[:, 0] = top[...]
    whole[:, 1:5] = block[...]
    whole[:, 5] = down[...]
    pair[0] = top[...]
    pair[1] = down[...]


def tick_body(token, out):
    out[...] = token[...]


def ordered(token, before, after):
    token, *_ = lax.optimization_barrier((token, *before))
    token = call(tick_body, jax.ShapeDtypeStruct((8, 128), F32), [VMEM], 10**11, 10**8)(token)
    return lax.optimization_barrier((token, *after))


def edges_of(*blocks):
    rows = jax.ShapeDtypeStruct((4 * len(blocks), 32, 512), BF16)
    first_rows, last_rows = call(edge_body, (rows, rows), [VMEM] * len(blocks), 0, 600_000)(*blocks)
    return shift(last_rows, "z", 1, False), shift(first_rows, "z", -1, False)


def states_body(start_state, rates, start, picked):
    place = position()
    source = lax.broadcasted_iota(jnp.int32, (512, 128), 0)
    lane = lax.broadcasted_iota(jnp.int32, (512, 128), 1)
    wanted = 64 * lax.shift_right_logical(lane, 4) + 16 * place[0] + jnp.bitwise_and(lane, 15)
    pick = (source == wanted).astype(F32)

    def of(value):
        return lax.dot_general(value, pick, NN, precision=lax.Precision.HIGHEST, preferred_element_type=F32)

    for part in range(2):
        start[:, part * 128 : part * 128 + 128] = of(start_state[:, :, part, :].reshape(128, 512))
    picked[...] = of(rates[...])


def pack_body(weight_in, weight_out, out, sems):
    place = position()
    rows = pl.ds(pl.multiple_of(16 * place[0], 16), 16)
    half = pl.ds(pl.multiple_of(256 * place[1], 128), 256)
    spans = [
        (weight_out.at[tap, :, rows, half], out.at[2:4, :, tap * 256 : tap * 256 + 256]) for tap in range(9)
    ]
    spans.append((weight_in.at[:, rows, pl.ds(pl.multiple_of(2304 * place[1], 128), 2304)], out.at[0:2]))
    copied(spans, sems)


def place_body(first, *refs):
    place = position()
    *pieces, out = refs
    for k, piece in enumerate(pieces):
        at = jnp.bitwise_and(place[3] - k + NZ, NZ - 1)
        begin = first if piece.shape[0] == 4 else 0
        for part in range(2):
            out[part, at] = piece[begin + part]


def placed(first, pieces):
    out = jax.ShapeDtypeStruct((2, NZ, 16, 2304), BF16)
    body = functools.partial(place_body, first)
    return call(body, out, [VMEM] * 8, 0, 0)(*pieces).reshape(2, 128, 2304)


def times(a_re, a_im, b_re, b_im):
    return a_re * b_re - a_im * b_im, a_re * b_im + a_im * b_re


def in_products(cells, weight, half):
    summed = []
    for b in range(3):
        total = None
        for a in range(3):
            tap = 3 * a + b
            first, last = max(tap * 512, 2304 * half), min(tap * 512 + 512, 2304 * half + 2304)
            if first >= last:
                continue
            window = cells[:, a : a + 4, :, first - tap * 512 : last - tap * 512].reshape(512, last - first)
            taps = weight[:, :, first - 2304 * half : last - 2304 * half].reshape(256, last - first)
            part = lax.dot_general(window, taps, NT, preferred_element_type=F32)
            total = part if total is None else total + part
        summed.append(total)
    return columns_shifted(summed)


def ahead_body(e0, weight, _, part):
    place = position()
    for half in range(2):

        @pl.when(place[1] == half)
        def _():
            part[...] = in_products(e0, weight, half)


def first_body(e0, e1, b2, h2, e3, weight, ahead, _, ext, part, sems):
    place = position()
    copies = {
        k: pltpu.make_async_copy(block, ext.at[k], sems.at[k]) for k, block in ((1, e1), (3, e3), (0, e0))
    }
    copies[2] = pltpu.make_async_copy(b2, ext.at[2, :, 1:5], sems.at[2])
    for copy in copies.values():
        copy.start()
    part[0] = ahead[...]
    ext[2, :, 0] = h2[0]
    ext[2, :, 5] = h2[1]
    for k in (1, 3, 2):
        copies[k].wait()
        for half in range(2):

            @pl.when(place[1] == half)
            def _():
                part[k] = in_products(ext.at[k], weight, half)

    copies[0].wait()


def second_body(ext, part, weight, start, table, local, tails):
    place = position()
    xi, ci, yi = place[0], place[1], place[2]
    lam_re, lam_im = table[0, 0:1, :], table[1, 0:1, :]

    def work(half):
        for k in range(NX):
            cells = ext.at[k]
            at = jnp.bitwise_and(xi - k + NX, NX - 1)
            driven = (part[k] + in_products(cells, weight, half)).reshape(4, 128, 256)
            first = jnp.logical_and(at == 0, jnp.logical_and(ci == 0, yi == 0))
            re = jnp.where(first, start[:, :128], 0.0)
            im = jnp.where(first, start[:, 128:], 0.0)
            for f in range(4):
                up_re, up_im = times(lam_re, lam_im, re, im)
                re, im = up_re + driven[f, :, :128], up_im + driven[f, :, 128:]
                local[k, f, :, :128] = re
                local[k, f, :, 128:] = im
            tails[at, :, :128] = re
            tails[at, :, 128:] = im

    for half in range(2):

        @pl.when(ci == 1 - half)
        def _():
            work(half)


def chain_body(own, other, table, total, entry):
    place = position()
    ci = place[1]
    lam_re, lam_im = table[0, 3:4, :], table[1, 3:4, :]
    re = im = jnp.zeros((128, 128), F32)
    low = ci == 0
    for x in range(NX):
        ours, theirs = own[x], other[x]
        before = (re, im)
        for c in range(NC):
            tail = jnp.where(low, ours, theirs) if c == 0 else jnp.where(low, theirs, ours)
            if c == 1:
                entry[x, :, :128] = jnp.where(low, before[0], re)
                entry[x, :, 128:] = jnp.where(low, before[1], im)
            up_re, up_im = times(lam_re, lam_im, re, im)
            re, im = up_re + tail[:, :128], up_im + tail[:, 128:]
    total[:, :128] = re.astype(BF16)
    total[:, 128:] = im.astype(BF16)


def held_body(local, entry, g1, g2, g3, table, held, first_row, last_row):
    place = position()
    def power(n):
        return table[0, pl.ds(n, 1), :], table[1, pl.ds(n, 1), :]

    re, im = g1[:, :128].astype(F32), g1[:, 128:].astype(F32)
    for g, n in ((g2, 4), (g3, 5)):
        more_re, more_im = times(*power(n), g[:, :128].astype(F32), g[:, 128:].astype(F32))
        re, im = re + more_re, im + more_im
    for k in range(NX):
        x = jnp.bitwise_and(place[0] - k + NX, NX - 1)
        to = SENT.index((NX - k) % NX)
        more_re, more_im = times(*power(6 + x), re, im)
        at_re, at_im = entry[x, :, :128] + more_re, entry[x, :, 128:] + more_im
        for f in range(4):
            up_re, up_im = times(*power(f), at_re, at_im)
            got_re = (local[k, f, :, :128] + up_re).astype(BF16)
            got_im = (local[k, f, :, 128:] + up_im).astype(BF16)
            held[to, f, :, :, :128] = got_re.reshape(4, 32, 128)
            held[to, f, :, :, 128:] = got_im.reshape(4, 32, 128)
            first_row[to, f, :, :128] = got_re[:32]
            first_row[to, f, :, 128:] = got_im[:32]
            last_row[to, f, :, :128] = got_re[96:]
            last_row[to, f, :, 128:] = got_im[96:]


def out_windows(edges, held, top, down, blocks):
    if edges:
        rows = [top[blocks][:, :, None]] + [held[blocks, :, n : n + 1] for n in range(4)] + [down[blocks][:, :, None]]
        windows = [jnp.concatenate([rows[a], rows[a + 3]], 2) for a in range(3)]
    else:
        windows = [held[blocks, :, a : a + 2] for a in range(3)]
    return [w.reshape(-1, 256) for w in windows]


def out_store(windows, w_own, w_other, outs):
    place = position()
    for ref, half in ((w_own, place[1]), (w_other, 1 - place[1])):
        first = pl.multiple_of(half * 256, 256)
        summed = []
        for b in range(3):
            total = None
            for a in range(3):
                tap = 3 * a + b
                weight = ref[:, :, tap * 256 : tap * 256 + 256].reshape(256, 256)
                part = lax.dot_general(windows[a], weight, NN, preferred_element_type=F32)
                total = part if total is None else total + part
            summed.append(total)
        value = columns_shifted(summed).reshape(-1, 4, 2, 32, 256)
        for k, out in enumerate(outs):
            out[:, :, :, pl.ds(first, 256)] = value[k].astype(out.dtype)


def inner_body(blocks, held, w_own, w_other, *outs):
    out_store(out_windows(False, held, None, None, blocks), w_own, w_other, outs)


def edge_out_body(held, top, down, w_own, w_other, *outs):
    out_store(out_windows(True, held, top, down, slice(1, 4)), w_own, w_other, outs)


def activated(mixing, skip, frames):
    pre = mixing + skip * frames.astype(F32)
    return (0.5 * pre * (1.0 + lax.erf(pre * 0.7071067811865476))).astype(BF16)


def own_body(held, top, down, w_own, w_other, frames, gain, i1, i2, i3, inner, edge, own):
    blocks = slice(0, 1)
    pairs = zip(out_windows(False, held, top, down, blocks), out_windows(True, held, top, down, blocks))
    out_store([jnp.concatenate(pair) for pair in pairs], w_own, w_other, (own, edge))
    skip = gain[...]
    for f in range(4):
        for row in range(2):
            mixing = own[f, row] + i1[f, row].astype(F32) + i2[f, row].astype(F32) + i3[f, row].astype(F32)
            inner[f, row] = activated(mixing, skip, frames[f, row + 1])


def last_body(frames, gain, inner, e0, e1, e2, e3, out):
    skip = gain[...]
    for f in range(4):
        out[f, 1:3] = inner[f]
        for row in range(2):
            mixing = e0[f, row] + e1[f, row].astype(F32) + e2[f, row].astype(F32) + e3[f, row].astype(F32)
            out[f, 3 * row] = activated(mixing, skip, frames[f, 3 * row])


def on_device(frames_in, weight_in, weight_out, log_decay, rotation, start_state, skip_gain):
    ci = lax.axis_index("c")
    piece = call(
        pack_body, jax.ShapeDtypeStruct((4, 16, 2304), BF16), [HBM, HBM], 0, 600_000,
        [pltpu.SemaphoreType.DMA((10,))],
    )(weight_in, weight_out)
    t0, d0 = edges_of(frames_in)
    up1, down1 = shift(piece, "z", 1), shift(piece, "z", -1)
    b2 = shift(frames_in, "x", 2)
    whole = jax.ShapeDtypeStruct((4, 6, 32, 512), BF16)
    e0, h0 = call(
        frame_body, (whole, jax.ShapeDtypeStruct((2, 4, 32, 512), BF16)), [VMEM] * 3, 0, 1_500_000
    )(frames_in, t0, d0)
    e1, e3 = shift(e0, "x", 1), shift(e0, "x", 3)
    token, up1, down1 = ordered(jnp.zeros((8, 128), F32), (up1, down1), (up1, down1))
    up2, down2 = shift(up1, "z", 1), shift(down1, "z", -1)
    start, picked = call(
        states_body,
        (jax.ShapeDtypeStruct((128, 256), F32), jax.ShapeDtypeStruct((2, 128), F32)),
        [VMEM] * 2, 40_000_000, 700_000,
    )(start_state, jnp.stack([log_decay, rotation]))
    steps = jnp.array([1, 2, 3, 4, 32, 64, 0, 8, 16, 24, 0, 0, 0, 0, 0, 0], F32)
    later = jnp.array([0, 0, 0, 0, 0, 0, 4, 4, 4, 4, 0, 0, 0, 0, 0, 0], F32)
    steps = (steps + later * ci.astype(F32))[:, None]
    size = jnp.exp(-picked[0:1] * steps)
    table = jnp.stack([size * jnp.cos(picked[1:2] * steps), size * jnp.sin(picked[1:2] * steps)])
    token, up2, down2, b2, h0, start, table = ordered(token, (up2, down2, b2, start, table), (up2, down2, b2, h0, start, table))
    up3, down3 = shift(up2, "z", 1), shift(down2, "z", -1)
    h2 = shift(h0, "x", 2)
    up4, down4 = shift(up3[0:2], "z", 1), shift(down3[2:4], "z", -1)

    up4, down4 = lax.optimization_barrier((up4, down4))
    near = (down3, down2, down1)
    win_own = placed(0, (piece, up1, up2, up3, up4, *near))
    win_other = shift(win_own, "c", 1)
    ahead = call(
        ahead_body, jax.ShapeDtypeStruct((512, 256), F32), [VMEM] * 3, 0, 0
    )(e0, win_own, token)
    token, ahead, e1, e3, h2 = ordered(token, (ahead, e1, e3, h2), (ahead, e1, e3, h2))
    ext, part = call(
        first_body,
        (jax.ShapeDtypeStruct((NX, 4, 6, 32, 512), BF16), jax.ShapeDtypeStruct((NX, 512, 256), F32)),
        [ANY, ANY, ANY, VMEM, ANY, VMEM, VMEM, VMEM],
        2_415_919_104, 9_000_000,
        [pltpu.SemaphoreType.DMA((NX,))],
    )(e0, e1, b2, h2, e3, win_own, ahead, token)
    local, tails = call(
        second_body,
        (jax.ShapeDtypeStruct((NX, 4, 128, 256), F32), jax.ShapeDtypeStruct((NX, 128, 256), F32)),
        [VMEM] * 5,
        2_415_919_104, 9_000_000,
    )(ext, part, win_other, start, table)

    other_tails = shift(tails, "c", 1)
    total, entry = call(
        chain_body,
        (jax.ShapeDtypeStruct((128, 256), BF16), jax.ShapeDtypeStruct((NX, 128, 256), F32)),
        [VMEM] * 3,
        4_000_000, 2_000_000,
    )(tails, other_tails, table)
    g1, g2, g3 = (shift(total, "y", k, False) for k in (1, 2, 3))
    total, down4 = lax.optimization_barrier((total, down4))
    wout_own = placed(2, (piece, up1, up2, up3, down4, *near))
    g1, g2, g3, wout_own = lax.optimization_barrier((g1, g2, g3, wout_own))
    wout_other = shift(wout_own, "c", 1)
    row = jax.ShapeDtypeStruct((NX, 4, 32, 256), BF16)
    held, first_row, last_row = call(
        held_body,
        (jax.ShapeDtypeStruct((NX, 4, 4, 32, 256), BF16), row, row),
        [VMEM] * 6,
        8_000_000, 4_000_000,
    )(local, entry, g1, g2, g3, table)

    half = (4, 2, 32, 512)

    def out_call(body, count, dtype, specs, flops):
        return call(
            body, (jax.ShapeDtypeStruct(half, dtype),) * count, [VMEM] * specs, flops, flops // 600
        )

    block = 603_979_776
    top, down = shift(last_row, "z", 1, False), shift(first_row, "z", -1, False)
    inner = out_call(functools.partial(inner_body, slice(1, 4)), 3, BF16, 3, 3 * block)(
        held, wout_own, wout_other
    )
    *inner, held = lax.optimization_barrier((*inner, held))
    inner = [shift(value, "x", k) for k, value in zip(SENT[1:], inner)]
    outer = out_call(edge_out_body, 3, BF16, 5, 30 * block)(held, top, down, wout_own, wout_other)
    *outer, held = lax.optimization_barrier((*outer, held))
    outer = [shift(value, "x", k) for k, value in zip(SENT[1:], outer)]
    *inner, held = lax.optimization_barrier((*inner, held))
    gain = skip_gain.reshape(1, 512)
    done, edge = call(
        own_body,
        (jax.ShapeDtypeStruct(half, BF16), jax.ShapeDtypeStruct(half, F32)),
        [VMEM] * 10, 0, 0,
        [pltpu.VMEM(half, F32)],
    )(held, top, down, wout_own, wout_other, frames_in, gain, *inner)
    return call(
        last_body,
        jax.ShapeDtypeStruct((4, 4, 32, 512), BF16),
        [VMEM] * 7,
        10_000_000, 5_000_000,
    )(frames_in, gain, done, edge, *outer)


def solution(mesh):
    fine = Mesh(mesh.devices.reshape(NY, NX, NC, NZ), ("y", "x", "c", "z"))
    frames = P(("y", "x", "c"), "z", None, None)
    return jax.shard_map(
        on_device,
        mesh=fine,
        in_specs=(frames, P(None, "z", None), P(None, None, "z", None), P(), P(), P("z", None, None, None), P()),
        out_specs=frames,
        check_vma=False,
    )
```
